256 devices in a mesh: rep: 32 (over y_hi, z, core), seq: 8 (over y_lo, x).
Axes of the slice: x: 4, y: 4 (y_hi: 2, y_lo: 2; y = y_hi * 2 + y_lo), z: 8, core: 2. Of those that a mesh axis runs over, the one named last changes fastest.
Arguments:
- text_tokens: bfloat16 [32, 512, 3072], P('rep', 'seq'), may hold values from -6 to 6
- image_tokens: bfloat16 [32, 576, 3072], P('rep', 'seq'), may hold values from -6 to 6
- weights: bfloat16 [2, 3072, 3, 3072], P(None, ('rep', 'seq'))
- qk_gain: float32 [2, 2, 128], replicated, may hold values from 0.5 to 4.2, as said below
- mod_table: float32 [28, 2, 2, 3072], replicated, may hold values from -3 to 3
- text_lengths: int32 [32], P('rep'), may hold values from 64 to 512, as said below
- time_index: int32 [32], P('rep'), may hold values from 0 to 27
Outputs:
- attended_text: bfloat16 [32, 512, 3072], P('rep', 'seq')
- attended_image: bfloat16 [32, 576, 3072], P('rep', 'seq')
The draws below stay inside these ranges and needn't reach their ends.
Inputs may be any that keep to these rules, and one draw needn't show every extreme that they name: `text_lengths`: padding of a prompt lies past its length; some prompt fills all 512 text tokens. `qk_gain`: positive gains.
All inputs are finite; a program needn't handle non-finite values.
Results may differ from the reference program's by a relative error of at most 0.01.
Values may be sent and summed in bfloat16 or wider, within the bound.
A program may use at most 128 MiB of HBM per device.

```python
import jax
import jax.numpy as jnp
from jax import lax

D = 3072
HEADS = 24
HD = 128
GRID = 24
TXT = 512
STEPS = 28
IMG = 576
REPLICAS = 32


def draw_weights(key, part):
    key = jax.random.fold_in(key, 11)
    base = jax.random.normal(key, (2, D, 3, D), jnp.float32) * D ** (-0.5)
    return base.astype(jnp.bfloat16)


def draw_qk_gain(key, part):
    key = jax.random.fold_in(key, 12)
    return jnp.exp(jax.random.uniform(key, (2, 2, HD), jnp.float32, -0.69, 0.69))


def draw_text_lengths(key, part):
    key = jax.random.fold_in(key, 13)
    first_key, second_key = jax.random.split(key)
    length_draw = jax.random.randint(first_key, (REPLICAS,), TXT // 8, TXT + 1)
    chosen = jax.random.randint(second_key, (), 0, REPLICAS)
    return jnp.where(jnp.arange(REPLICAS) == chosen, TXT, length_draw).astype(jnp.int32)


def touch_ends(array, own_key, low, top_value):
    extent = array.shape
    place = [jax.random.randint(jax.random.fold_in(own_key, axis), (), 0, extent[axis]) for axis in range(len(extent))]
    array = array.at[tuple(place)].set(low)
    longest = extent.index(max(extent))
    place[longest] = (place[longest] + 1) % extent[longest]
    return array.at[tuple(place)].set(top_value)


def shard_levels(own_key, shape, cuts, smallest, largest):
    loudness = 1.0
    for dim, parts in cuts:
        steps = jax.random.uniform(jax.random.fold_in(jax.random.fold_in(own_key, 6), dim), (parts,), jnp.float32, smallest / len(cuts), largest / len(cuts))
        loudness = loudness * jnp.repeat(jnp.exp(steps), shape[dim] // parts).reshape((-1,) + (1,) * (len(shape) - 1 - dim))
    return loudness


def noise(own_key, extent, deviation, most, shards=(), kind=jnp.bfloat16):
    entries = jax.random.normal(own_key, extent, jnp.float32) * deviation
    if len(shards) > 0:
        entries = shard_levels(own_key, extent, shards, -0.22, 0.18) * entries
    return jnp.clip(entries, min=-most, max=most).astype(kind)


def setup_inputs(seed: int = 0) -> dict:
    key_of = jax.random.split(jax.random.key(seed), 8)
    text_tokens = noise(key_of[0], (REPLICAS, TXT, D), 1.0, 6.0, ((0, 32), (1, 8)))
    image_tokens = noise(key_of[1], (REPLICAS, IMG, D), 1.0, 6.0, ((0, 32), (1, 8)))
    weights = draw_weights(jax.random.fold_in(key_of[7], 71), 0)
    qk_gain = draw_qk_gain(jax.random.fold_in(key_of[7], 71), 0)
    mod_table = noise(key_of[4], (STEPS, 2, 2, D), 0.5, 3.0, (), jnp.float32)
    text_lengths = draw_text_lengths(jax.random.fold_in(key_of[7], 71), 0)
    time_index = touch_ends(jax.random.randint(key_of[6], (REPLICAS,), 0, STEPS), jax.random.fold_in(key_of[6], 1), 0, STEPS - 1).astype(jnp.int32)
    return dict(text_tokens=text_tokens, image_tokens=image_tokens, weights=weights, qk_gain=qk_gain, mod_table=mod_table, text_lengths=text_lengths, time_index=time_index)


def layer_modulate(tokens, shift_row, scale_row):
    values = tokens.astype(jnp.float32)
    center = values - lax.optimization_barrier(jnp.mean(values, axis=-1, keepdims=True))
    spread = lax.optimization_barrier(jnp.mean(center * center, axis=-1, keepdims=True))
    normed = center * lax.rsqrt(spread + 1e-06)
    return (normed * (1.0 + shift_row * 0.0 + scale_row) + shift_row).astype(jnp.bfloat16)

def rope_tables(length, text_count, grid_side, head_dim):
    pair_count = head_dim // 2
    still_pairs = head_dim // 16
    row_pairs = (pair_count - still_pairs) // 2
    col_pairs = pair_count - still_pairs - row_pairs
    position = jnp.arange(length, dtype=jnp.int32)
    image_pos = jnp.maximum(position - text_count, 0)
    is_image = (position >= text_count).astype(jnp.float32)
    row_pos = (image_pos // grid_side).astype(jnp.float32) * is_image
    col_pos = (image_pos % grid_side).astype(jnp.float32) * is_image
    row_freq = 10000.0 ** (-jnp.arange(row_pairs, dtype=jnp.float32) / row_pairs)
    col_freq = 10000.0 ** (-jnp.arange(col_pairs, dtype=jnp.float32) / col_pairs)
    angles = jnp.concatenate([jnp.zeros((length, still_pairs), jnp.float32), row_pos[:, None] * row_freq[None, :], col_pos[:, None] * col_freq[None, :]], axis=1)
    return (jnp.cos(angles), jnp.sin(angles))

def rotate(values, cosine, sine):
    shaped = values.reshape(values.shape[0], values.shape[1], -1, 2)
    first_part = shaped[..., 0]
    second_part = shaped[..., 1]
    cos_part = cosine[:, None, :]
    sin_part = sine[:, None, :]
    turned = jnp.stack([first_part * cos_part - second_part * sin_part, first_part * sin_part + second_part * cos_part], axis=-1)
    return turned.reshape(values.shape)

def normalize_heads(values, gain):
    power = lax.optimization_barrier(jnp.mean(values * values, axis=-1, keepdims=True))
    return values * lax.rsqrt(power + 1e-06) * gain

def prepare_heads(projected, gain, cosine, sine):
    query = rotate(normalize_heads(projected[:, 0], gain[0]), cosine, sine).astype(jnp.bfloat16)
    key_part = rotate(normalize_heads(projected[:, 1], gain[1]), cosine, sine).astype(jnp.bfloat16)
    value_part = projected[:, 2].astype(jnp.bfloat16)
    return (query, key_part, value_part)

def attend_head(query_head, key_head, value_head, allowed):
    scores = lax.dot_general(query_head, key_head, (((1,), (1,)), ((), ())), preferred_element_type=jnp.float32)
    scores = scores * query_head.shape[-1] ** (-0.5)
    scores = jnp.where(allowed[None, :], scores, -jnp.inf)
    row_max = lax.optimization_barrier(jnp.max(scores, axis=-1, keepdims=True))
    exponent = jnp.exp(scores - row_max)
    softmax_out = (exponent / lax.optimization_barrier(jnp.sum(exponent, axis=-1, keepdims=True))).astype(jnp.bfloat16)
    return jnp.dot(softmax_out, value_head, preferred_element_type=jnp.float32).astype(jnp.bfloat16)

def run_attention(queries, keys_all, values_all, allowed):

    def one_head(trio):
        return attend_head(trio[0], trio[1], trio[2], allowed)
    stacked = (jnp.moveaxis(queries, 1, 0), jnp.moveaxis(keys_all, 1, 0), jnp.moveaxis(values_all, 1, 0))
    outputs = lax.map(one_head, stacked)
    outputs = jnp.moveaxis(outputs, 0, 1)
    return outputs.reshape(outputs.shape[0], -1)

def reference(text_tokens, image_tokens, weights, qk_gain, mod_table, text_lengths, time_index):
    total_rows = TXT + IMG
    cosine_all, sine_all = rope_tables(total_rows, TXT, GRID, HD)
    position = jnp.arange(total_rows, dtype=jnp.int32)

    def one_sample(operands):
        text_rows, image_rows, live_count, step_index = operands
        table_row = lax.dynamic_index_in_dim(mod_table, step_index, 0, keepdims=False)
        prepared = []
        for stream in range(2):
            rows_here = (text_rows, image_rows)[stream]
            modded = layer_modulate(rows_here, table_row[stream, 0], table_row[stream, 1])
            flat_weight = weights[stream].reshape(D, 3 * D)
            projected = jnp.dot(modded, flat_weight, preferred_element_type=jnp.float32)
            row_count = rows_here.shape[0]
            offset_rows = 0 if stream == 0 else TXT
            projected = projected.reshape(row_count, 3, HEADS, HD)
            prepared.append(prepare_heads(projected, qk_gain[stream], cosine_all[offset_rows:offset_rows + row_count], sine_all[offset_rows:offset_rows + row_count]))
        queries = jnp.concatenate([prepared[0][0], prepared[1][0]], axis=0)
        keys_all = jnp.concatenate([prepared[0][1], prepared[1][1]], axis=0)
        values_all = jnp.concatenate([prepared[0][2], prepared[1][2]], axis=0)
        allowed = (position >= TXT) | (position < live_count)
        joined = run_attention(queries, keys_all, values_all, allowed)
        return (joined[:TXT], joined[TXT:])
    return lax.map(one_sample, (text_tokens, image_tokens, text_lengths.astype(jnp.int32), time_index.astype(jnp.int32)))
```

```python
import functools

import jax
import jax.numpy as jnp
import numpy as np
from jax import lax
from jax.experimental import pallas as pl
from jax.experimental.pallas import tpu as pltpu
from jax.sharding import PartitionSpec as P

D = 3072
HD = 128
GRID = 24
TXT = 512
IMG = GRID * GRID
TOTAL = TXT + IMG
SEQ = 8
NZ = 8
HEADS_HERE = 3
TROWS = TXT // SEQ
IROWS = IMG // SEQ
REST = IROWS - 64
WROWS = 12
KSTEP = 768
SCALE = float(HD**-0.5 * np.log2(np.e))
MESH = pl.DeviceIdType.MESH
BF16, F32 = jnp.bfloat16, jnp.float32


def rope_rows():
    pairs, still = HD // 2, HD // 16
    rows = (pairs - still) // 2
    cols = pairs - still - rows
    place = np.concatenate(
        [
            (np.arange(SEQ)[:, None] * IROWS + np.arange(64)[None, :]).reshape(-1),
            (np.arange(SEQ)[:, None] * IROWS + 64 + np.arange(REST)[None, :]).reshape(-1),
        ]
    )
    row_pos = (place // GRID).astype(np.float32)
    col_pos = (place % GRID).astype(np.float32)
    row_freq = (10000.0 ** (-np.arange(rows) / rows)).astype(np.float32)
    col_freq = (10000.0 ** (-np.arange(cols) / cols)).astype(np.float32)
    angles = np.concatenate(
        [
            np.zeros((IMG, still), np.float32),
            row_pos[:, None] * row_freq[None, :],
            col_pos[:, None] * col_freq[None, :],
        ],
        axis=1,
    )
    cosine = np.repeat(np.cos(angles), 2, axis=1)
    sine = np.repeat(np.sin(angles), 2, axis=1)
    sine[:, 0::2] *= -1.0
    return cosine.astype(np.float32), sine.astype(np.float32)


def kernel(
    wsrc, text, image, mods, gains, cosine, sine, length,
    out,
    W, A, T, RM, XR, acc, Q, K, V, OB, bias, sel,
    a2a_s, a2a_r, y_s, y_r, zr_s, zr_r, zl_s, zl_r, sib_s, sib_r, tok_s, tok_r, out_s, out_r, own_sem,
):
    R, S = lax.axis_index("rep"), lax.axis_index("seq")
    core = lax.rem(R, 2)
    z = lax.rem(R // 2, NZ)
    yh = R // (2 * NZ)
    x = lax.rem(S, 4)
    yl = S // 4

    def rep_of(y, zz, c):
        return (y * NZ + zz) * 2 + c

    def up(dz):
        return lax.rem(z + dz + NZ, NZ)

    def xs(dx, row):
        return row * 4 + lax.rem(x + dx + 4, 4)

    sib = (rep_of(yh, z, 1 - core), S)
    zr = (rep_of(yh, up(1), core), S)
    zl = (rep_of(yh, up(-1), core), S)
    yp = (rep_of(1 - yh, z, core), S)
    peers = [(R, lax.rem(S + d, SEQ)) for d in range(1, SEQ)]
    s_yp, s_xr, s_xl, s_xx = xs(0, 1 - yl), xs(1, yl), xs(-1, yl), xs(2, yl)
    o_xr, o_xl, o_xx = xs(1, 1 - yl), xs(-1, 1 - yl), xs(2, 1 - yl)

    barrier = pltpu.get_barrier_semaphore()
    partners = [sib, zr, zl, yp] + peers
    for device in partners:
        pl.semaphore_signal(barrier, inc=1, device_id=device, device_id_type=MESH)
    pl.semaphore_wait(barrier, len(partners))

    pending = []

    def send(src, dst, ssem, rsem, device):
        copy = pltpu.make_async_remote_copy(
            src_ref=src, dst_ref=dst, send_sem=ssem, recv_sem=rsem, device_id=device, device_id_type=MESH
        )
        copy.start()
        pending.append(copy)

    def arrived(dst, ssem, rsem, device):
        pltpu.make_async_remote_copy(
            src_ref=dst, dst_ref=dst, send_sem=ssem, recv_sem=rsem, device_id=device, device_id_type=MESH
        ).wait_recv()

    def slot(j, s):
        return A.at[j, :, :, pl.ds(pl.multiple_of(s * 16, 16), 16), :]

    def piece(j, g):
        return wsrc.at[:, :, :, pl.ds(pl.multiple_of(g * (HEADS_HERE * HD) + j * HD, HD), HD)]

    def a2a_start(j):
        for d in range(1, SEQ):
            send(piece(j, peers[d - 1][1]), slot(j, S), a2a_s.at[j, d - 1], a2a_r.at[j, d - 1], peers[d - 1])
        copy = pltpu.make_async_copy(piece(j, S), slot(j, S), own_sem.at[j])
        copy.start()
        return copy

    own_copies = [a2a_start(0)]

    def modulate(rows, stream):
        v = rows.astype(F32)
        center = v - jnp.mean(v, axis=-1, keepdims=True)
        spread = jnp.mean(center * center, axis=-1, keepdims=True)
        normed = center * lax.rsqrt(spread + 1e-06)
        return normed * (1.0 + mods[2 * stream + 1 : 2 * stream + 2, :]) + mods[2 * stream : 2 * stream + 1, :]

    def mod_text(i, carry):
        rows = pl.ds(pl.multiple_of(i * 16, 16), 16)
        T[S, rows, :] = modulate(text[rows, :], 0).astype(BF16)
        return carry

    def mod_image(i, carry):
        rows = pl.ds(pl.multiple_of(i * 16, 16), 16)
        T[S, pl.ds(pl.multiple_of(64 + i * 16, 16), 16), :] = modulate(image[rows, :], 1).astype(BF16)
        return carry

    lax.fori_loop(0, 4, mod_text, 0)
    lax.fori_loop(0, 4, mod_image, 0)
    rest = modulate(image[64:72, :], 1)
    RM[S] = jnp.concatenate([rest[:, : D // 2], rest[:, D // 2 :]], axis=0).astype(BF16)

    def send_tokens(s, first, device):
        send(T.at[s], T.at[s], tok_s.at[first], tok_r.at[first], device)
        send(RM.at[s], RM.at[s], tok_s.at[first + 1], tok_r.at[first + 1], device)

    def tokens_arrived(s, first, device):
        arrived(T.at[s], tok_s.at[first], tok_r.at[first], device)
        arrived(RM.at[s], tok_s.at[first + 1], tok_r.at[first + 1], device)

    d_yp, d_xr, d_xl = (R, s_yp), (R, s_xr), (R, s_xl)
    send_tokens(S, 0, d_xr)
    send_tokens(S, 2, d_xl)
    send_tokens(S, 4, d_yp)
    own_copies.append(a2a_start(1))
    own_copies.append(a2a_start(2))

    i96 = lax.broadcasted_iota(jnp.int32, (96, 128), 0)
    i128 = lax.broadcasted_iota(jnp.int32, (96, 128), 1)
    sel[...] = jnp.where(i128 == (i96 // WROWS) * 16 + lax.rem(i96, WROWS), 1.0, 0.0).astype(BF16)
    where = lax.broadcasted_iota(jnp.int32, (8, TXT), 1)
    bias[...] = jnp.where(where < length[0], 0.0, -jnp.inf).astype(F32)

    def rows_of(zz, c):
        return pl.ds(pl.multiple_of((zz * 2 + c) * 96, 32), 96)

    def block(j, y, zz, c):
        return W.at[j, :, y, rows_of(zz, c), :]

    def half(j, st, y, zz, c):
        return W.at[j, st, y, rows_of(zz, c), :]

    def gather_rows(j):
        own_copies[j].wait()
        for d in range(1, SEQ):
            src = lax.rem(S + SEQ - d, SEQ)
            arrived(slot(j, src), a2a_s.at[j, d - 1], a2a_r.at[j, d - 1], peers[d - 1])
        for st in range(2):
            rows = jnp.concatenate([A[j, st, q] for q in range(3)], axis=1)
            W[j, st, yh, rows_of(z, core), :] = jnp.dot(sel[...], rows, preferred_element_type=F32).astype(BF16)

    yy = [yh, 1 - yh]

    def sib_send(j, w, k, zz):
        b = block(j, yy[w], zz, core)
        send(b, b, sib_s.at[j, w, k], sib_r.at[j, w, k], sib)

    def begin(j):
        gather_rows(j)
        b = block(j, yh, z, core)
        send(b, b, y_s.at[j], y_r.at[j], yp)
        send(b, b, zr_s.at[j, 0, 0], zr_r.at[j, 0, 0], zr)
        send(b, b, zl_s.at[j, 0, 0], zl_r.at[j, 0, 0], zl)
        sib_send(j, 0, 0, z)

    def begin_partner(j):
        b = block(j, 1 - yh, z, core)
        arrived(b, y_s.at[j], y_r.at[j], yp)
        send(b, b, zr_s.at[j, 1, 0], zr_r.at[j, 1, 0], zr)
        send(b, b, zl_s.at[j, 1, 0], zl_r.at[j, 1, 0], zl)
        sib_send(j, 1, 0, z)

    def hop(j, w, step):
        y = yy[w]
        if step < 4:
            b = block(j, y, up(-step), core)
            arrived(b, zr_s.at[j, w, step - 1], zr_r.at[j, w, step - 1], zr)
            f = b if step < 3 else half(j, 0, y, up(-step), core)
            send(f, f, zr_s.at[j, w, step], zr_r.at[j, w, step], zr)
            sib_send(j, w, step, up(-step))
            b = block(j, y, up(step), core)
            arrived(b, zl_s.at[j, w, step - 1], zl_r.at[j, w, step - 1], zl)
            f = b if step < 3 else half(j, 1, y, up(step), core)
            send(f, f, zl_s.at[j, w, step], zl_r.at[j, w, step], zl)
            sib_send(j, w, step + 3, up(step))
        else:
            arrived(half(j, 0, y, up(4), core), zr_s.at[j, w, 3], zr_r.at[j, w, 3], zr)
            arrived(half(j, 1, y, up(4), core), zl_s.at[j, w, 3], zl_r.at[j, w, 3], zl)
            sib_send(j, w, 7, up(4))

    def sib_arrived(j):
        for w in range(2):
            for k, dz in enumerate((0, -1, -2, -3, 1, 2, 3, 4)):
                arrived(block(j, yy[w], up(dz), 1 - core), sib_s.at[j, w, k], sib_r.at[j, w, k], sib)

    def project(j, st):
        n = TXT if st == 0 else IMG
        acc[0:n, :] = jnp.zeros((n, 3 * HD), F32)

        def body(k, carry):
            cols = pl.ds(pl.multiple_of(k * KSTEP, KSTEP), KSTEP)
            lhs = T[:, 64 * st : 64 * st + 64, cols].reshape(SEQ * 64, KSTEP)
            if st == 1:
                lhs = jnp.concatenate([lhs, XR[:, cols]], axis=0)
            rhs = W[j, st, k // 2, pl.ds(pl.multiple_of(lax.rem(k, 2) * KSTEP, KSTEP), KSTEP), :]
            acc[0:n, :] += jnp.dot(lhs, rhs, preferred_element_type=F32)
            return carry

        lax.fori_loop(0, D // KSTEP, body, 0)

    even = lax.rem(lax.broadcasted_iota(jnp.int32, (64, HD), 1), 2) == 0

    def finish(st):
        base = 0 if st == 0 else TXT

        def body(i, carry):
            here = pl.ds(pl.multiple_of(i * 64, 64), 64)
            there = pl.ds(pl.multiple_of(base + i * 64, 64), 64)
            for part, store in ((0, Q), (1, K)):
                v = acc[here, part * HD : (part + 1) * HD]
                power = jnp.mean(v * v, axis=-1, keepdims=True)
                v = v * lax.rsqrt(power + 1e-06) * gains[2 * st + part : 2 * st + part + 1, :]
                if st == 1:
                    turned = jnp.where(even, pltpu.roll(v, HD - 1, 1), pltpu.roll(v, 1, 1))
                    v = v * cosine[here, :] + turned * sine[here, :]
                store[there, :] = v.astype(BF16)
            V[there, :] = acc[here, 2 * HD : 3 * HD].astype(BF16)
            return carry

        lax.fori_loop(0, (TXT if st == 0 else IMG) // 64, body, 0)

    def attend(q):
        scores = lax.dot_general(q, K[...], (((1,), (1,)), ((), ())), preferred_element_type=F32) * SCALE
        scores = jnp.concatenate([scores[:, :TXT] + bias[0:1, :], scores[:, TXT:]], axis=1)
        weight = jnp.exp2(scores - jnp.max(scores, axis=-1, keepdims=True))
        total = jnp.sum(weight, axis=-1, keepdims=True)
        return jnp.dot(weight.astype(BF16), V[...], preferred_element_type=F32) / total

    def attend_full(j, st):
        def body(i, carry):
            o = attend(Q[pl.ds(pl.multiple_of(st * 512 + i * 256, 256), 256), :])
            OB[j, pl.ds(i * 4, 4), 64 * st : 64 * st + 64, :] = o.astype(BF16).reshape(4, 64, HD)
            return carry

        lax.fori_loop(0, 2, body, 0)

    def attend_rest(j):
        o = attend(Q[1024:1088, :]).reshape(SEQ, REST, HD)
        OB[j, :, 128:144, :] = jnp.concatenate([o, jnp.zeros_like(o)], axis=1).astype(BF16)

    def give(j):
        lanes = pl.ds(pl.multiple_of((S * HEADS_HERE + j) * HD, HD), HD)
        for d in range(1, SEQ):
            send(OB.at[j, peers[d - 1][1]], out.at[:, lanes], out_s.at[j, d - 1], out_r.at[j, d - 1], peers[d - 1])
        out[:, lanes] = OB[j, S]

    def take(j):
        for d in range(1, SEQ):
            src = lax.rem(S + SEQ - d, SEQ)
            lanes = pl.ds(pl.multiple_of((src * HEADS_HERE + j) * HD, HD), HD)
            arrived(out.at[:, lanes], out_s.at[j, d - 1], out_r.at[j, d - 1], peers[d - 1])

    def parts_of(j):
        return [
            lambda: (sib_arrived(j), project(j, 0), finish(0)),
            lambda: (project(j, 1), finish(1)),
            lambda: attend_full(j, 0),
            lambda: (attend_full(j, 1), attend_rest(j), give(j)),
        ]

    begin(0)
    begin_partner(0)
    for step in (1, 2):
        for w in (0, 1):
            hop(0, w, step)
    tokens_arrived(s_xl, 0, d_xr)
    send(T.at[s_xl, 0:64], T.at[s_xl, 0:64], tok_s.at[6], tok_r.at[6], d_xr)
    tokens_arrived(s_xr, 2, d_xl)
    send(T.at[s_xr, 64:128], T.at[s_xr, 64:128], tok_s.at[7], tok_r.at[7], d_xl)
    send(RM.at[s_xr], RM.at[s_xr], tok_s.at[8], tok_r.at[8], d_xl)
    tokens_arrived(s_yp, 4, d_yp)
    send_tokens(s_yp, 9, d_xr)
    send_tokens(s_yp, 11, d_xl)
    for w in (0, 1):
        hop(0, w, 3)
    begin(1)
    begin_partner(1)
    for w in (0, 1):
        hop(0, w, 4)
    for w in (0, 1):
        hop(1, w, 1)
    arrived(T.at[s_xx, 0:64], tok_s.at[6], tok_r.at[6], d_xr)
    arrived(T.at[s_xx, 64:128], tok_s.at[7], tok_r.at[7], d_xl)
    arrived(RM.at[s_xx], tok_s.at[8], tok_r.at[8], d_xl)
    send_tokens(s_xx, 13, d_yp)
    for step in (2, 3):
        for w in (0, 1):
            hop(1, w, step)
    begin(2)
    begin_partner(2)
    tokens_arrived(o_xl, 9, d_xr)
    tokens_arrived(o_xr, 11, d_xl)
    tokens_arrived(o_xx, 13, d_yp)

    def unpack(i, carry):
        pair = [RM[2 * i + n].astype(F32) for n in range(2)]
        rows = [jnp.concatenate([p[0:8], p[8:16]], axis=1) for p in pair]
        XR[pl.ds(pl.multiple_of(i * 16, 16), 16), :] = jnp.concatenate(rows, axis=0).astype(BF16)
        return carry

    lax.fori_loop(0, 4, unpack, 0)
    for w in (0, 1):
        hop(1, w, 4)
    todo = parts_of(0) + parts_of(1)
    for step in (1, 2, 3, 4):
        for w in (0, 1):
            if todo:
                todo.pop(0)()
            hop(2, w, step)
    for part in todo + parts_of(2):
        part()
    for j in range(HEADS_HERE):
        take(j)
    for copy in pending:
        copy.wait_send()


def on_device(text_tokens, image_tokens, weights, qk_gain, mod_table, text_lengths, time_index):
    mods = lax.dynamic_index_in_dim(mod_table, time_index[0], 0, keepdims=False).reshape(4, D)
    wsrc = jnp.pad(jnp.swapaxes(weights, 1, 2), ((0, 0), (0, 0), (0, 16 - WROWS), (0, 0)))
    cosine, sine = rope_rows()
    vmem = pl.BlockSpec(memory_space=pltpu.VMEM)
    dma = pltpu.SemaphoreType.DMA
    n_tok = 15
    result = pl.pallas_call(
        kernel,
        out_shape=jax.ShapeDtypeStruct((144, D), BF16),
        in_specs=[vmem] * 7 + [pl.BlockSpec(memory_space=pltpu.SMEM)],
        out_specs=vmem,
        scratch_shapes=[
            pltpu.VMEM((HEADS_HERE, 2, 2, D // 2, 3 * HD), BF16),
            pltpu.VMEM((HEADS_HERE, 2, 3, 128, HD), BF16),
            pltpu.VMEM((SEQ, 128, D), BF16),
            pltpu.VMEM((SEQ, 16, D // 2), BF16),
            pltpu.VMEM((SEQ * REST, D), BF16),
            pltpu.VMEM((IMG, 3 * HD), F32),
            pltpu.VMEM((TOTAL, HD), BF16),
            pltpu.VMEM((TOTAL, HD), BF16),
            pltpu.VMEM((TOTAL, HD), BF16),
            pltpu.VMEM((HEADS_HERE, SEQ, 144, HD), BF16),
            pltpu.VMEM((8, TXT), F32),
            pltpu.VMEM((96, 128), BF16),
            dma((3, 7)), dma((3, 7)),
            dma((3,)), dma((3,)),
            dma((3, 2, 4)), dma((3, 2, 4)),
            dma((3, 2, 4)), dma((3, 2, 4)),
            dma((3, 2, 8)), dma((3, 2, 8)),
            dma((n_tok,)), dma((n_tok,)),
            dma((3, 7)), dma((3, 7)),
            dma((3,)),
        ],
        compiler_params=pltpu.CompilerParams(
            collective_id=0, has_side_effects=True, vmem_limit_bytes=56 * 1024 * 1024
        ),
        cost_estimate=pl.CostEstimate(flops=9_500_000_000, bytes_accessed=30_000_000, transcendentals=3_600_000),
        name="joint_attention",
    )(
        wsrc, text_tokens[0], image_tokens[0], mods, qk_gain.reshape(4, HD),
        jnp.asarray(cosine), jnp.asarray(sine), text_lengths.astype(jnp.int32),
    )
    return result[None, :TROWS], result[None, TROWS : TROWS + IROWS]


def solution(mesh):
    placed = (
        P("rep", "seq", None),
        P("rep", "seq", None),
        P(None, ("rep", "seq"), None, None),
        P(),
        P(),
        P("rep"),
        P("rep"),
    )
    return jax.shard_map(
        on_device,
        mesh=mesh,
        in_specs=placed,
        out_specs=(P("rep", "seq", None), P("rep", "seq", None)),
        check_vma=False,
    )
```

```python
import functools

import jax
import jax.numpy as jnp
import numpy as np
from jax import lax
from jax.experimental import pallas as pl
from jax.experimental.pallas import tpu as pltpu
from jax.sharding import PartitionSpec as P

D = 3072
HD = 128
GRID = 24
TXT = 512
IMG = GRID * GRID
TOTAL = TXT + IMG
SEQ = 8
NZ = 8
HEADS_HERE = 3
TROWS = TXT // SEQ
IROWS = IMG // SEQ
REST = IROWS - 64
WROWS = 12
KSTEP = 768
SCALE = float(HD**-0.5 * np.log2(np.e))
MESH = pl.DeviceIdType.MESH
BF16, F32 = jnp.bfloat16, jnp.float32


def rope_rows():
    pairs, still = HD // 2, HD // 16
    rows = (pairs - still) // 2
    cols = pairs - still - rows
    place = np.concatenate(
        [
            (np.arange(SEQ)[:, None] * IROWS + np.arange(64)[None, :]).reshape(-1),
            (np.arange(SEQ)[:, None] * IROWS + 64 + np.arange(REST)[None, :]).reshape(-1),
        ]
    )
    row_pos = (place // GRID).astype(np.float32)
    col_pos = (place % GRID).astype(np.float32)
    row_freq = (10000.0 ** (-np.arange(rows) / rows)).astype(np.float32)
    col_freq = (10000.0 ** (-np.arange(cols) / cols)).astype(np.float32)
    angles = np.concatenate(
        [
            np.zeros((IMG, still), np.float32),
            row_pos[:, None] * row_freq[None, :],
            col_pos[:, None] * col_freq[None, :],
        ],
        axis=1,
    )
    cosine = np.repeat(np.cos(angles), 2, axis=1)
    sine = np.repeat(np.sin(angles), 2, axis=1)
    sine[:, 0::2] *= -1.0
    return cosine.astype(np.float32), sine.astype(np.float32)


def kernel(
    wraw, text, image, mods, gains, cosine, sine, length,
    out,
    wsrc, W, A, T, RM, XR, Q, K, V, OB, bias, sel,
    a2a_s, a2a_r, y_s, y_r, zr_s, zr_r, zl_s, zl_r, sib_s, sib_r, tok_s, tok_r, out_s, out_r, own_sem,
):
    R, S = lax.axis_index("rep"), lax.axis_index("seq")
    core = lax.rem(R, 2)
    z = lax.rem(R // 2, NZ)
    yh = R // (2 * NZ)
    x = lax.rem(S, 4)
    yl = S // 4

    def rep_of(y, zz, c):
        return (y * NZ + zz) * 2 + c

    def up(dz):
        return lax.rem(z + dz + NZ, NZ)

    def xs(dx, row):
        return row * 4 + lax.rem(x + dx + 4, 4)

    sib = (rep_of(yh, z, 1 - core), S)
    zr = (rep_of(yh, up(1), core), S)
    zl = (rep_of(yh, up(-1), core), S)
    yp = (rep_of(1 - yh, z, core), S)
    peers = [(R, lax.rem(S + d, SEQ)) for d in range(1, SEQ)]
    s_yp, s_xr, s_xl, s_xx = xs(0, 1 - yl), xs(1, yl), xs(-1, yl), xs(2, yl)
    o_xr, o_xl, o_xx = xs(1, 1 - yl), xs(-1, 1 - yl), xs(2, 1 - yl)

    wsrc[:, :, 0:WROWS, :] = wraw[...]
    wsrc[:, :, WROWS:16, :] = jnp.zeros((2, 3, 16 - WROWS, D), BF16)

    barrier = pltpu.get_barrier_semaphore()
    partners = [sib, zr, zl, yp] + peers
    for device in partners:
        pl.semaphore_signal(barrier, inc=1, device_id=device, device_id_type=MESH)
    pl.semaphore_wait(barrier, len(partners))

    pending = []

    def send(src, dst, ssem, rsem, device):
        copy = pltpu.make_async_remote_copy(
            src_ref=src, dst_ref=dst, send_sem=ssem, recv_sem=rsem, device_id=device, device_id_type=MESH
        )
        copy.start()
        pending.append(copy)

    def arrived(dst, ssem, rsem, device):
        pltpu.make_async_remote_copy(
            src_ref=dst, dst_ref=dst, send_sem=ssem, recv_sem=rsem, device_id=device, device_id_type=MESH
        ).wait_recv()

    def slot(j, s):
        return A.at[j, :, :, pl.ds(pl.multiple_of(s * 16, 16), 16), :]

    def piece(j, g):
        return wsrc.at[:, :, :, pl.ds(pl.multiple_of(g * (HEADS_HERE * HD) + j * HD, HD), HD)]

    def a2a_start(j):
        for d in range(1, SEQ):
            send(piece(j, peers[d - 1][1]), slot(j, S), a2a_s.at[j, d - 1], a2a_r.at[j, d - 1], peers[d - 1])
        copy = pltpu.make_async_copy(piece(j, S), slot(j, S), own_sem.at[j])
        copy.start()
        return copy

    own_copies = [a2a_start(0)]

    def modulate(rows, stream):
        v = rows.astype(F32)
        center = v - jnp.mean(v, axis=-1, keepdims=True)
        spread = jnp.mean(center * center, axis=-1, keepdims=True)
        normed = center * lax.rsqrt(spread + 1e-06)
        return normed * (1.0 + mods[stream, 1:2, :]) + mods[stream, 0:1, :]

    def mod_text(i, carry):
        rows = pl.ds(pl.multiple_of(i * 16, 16), 16)
        T[S, rows, :] = modulate(text[rows, :], 0).astype(BF16)
        return carry

    def mod_image(i, carry):
        rows = pl.ds(pl.multiple_of(i * 16, 16), 16)
        T[S, pl.ds(pl.multiple_of(64 + i * 16, 16), 16), :] = modulate(image[rows, :], 1).astype(BF16)
        return carry

    lax.fori_loop(0, 4, mod_text, 0)
    lax.fori_loop(0, 4, mod_image, 0)
    rest = modulate(image[64:72, :], 1)
    RM[S] = jnp.concatenate([rest[:, : D // 2], rest[:, D // 2 :]], axis=0).astype(BF16)

    def send_tokens(s, first, device):
        send(T.at[s], T.at[s], tok_s.at[first], tok_r.at[first], device)
        send(RM.at[s], RM.at[s], tok_s.at[first + 1], tok_r.at[first + 1], device)

    def tokens_arrived(s, first, device):
        arrived(T.at[s], tok_s.at[first], tok_r.at[first], device)
        arrived(RM.at[s], tok_s.at[first + 1], tok_r.at[first + 1], device)

    own_copies.append(a2a_start(1))
    own_copies.append(a2a_start(2))
    d_yp, d_xr, d_xl = (R, s_yp), (R, s_xr), (R, s_xl)
    i96 = lax.broadcasted_iota(jnp.int32, (96, 128), 0)
    i128 = lax.broadcasted_iota(jnp.int32, (96, 128), 1)
    sel[...] = jnp.where(i128 == (i96 // WROWS) * 16 + lax.rem(i96, WROWS), 1.0, 0.0).astype(BF16)
    where = lax.broadcasted_iota(jnp.int32, (8, TXT), 1)
    bias[...] = jnp.where(where < length[0], 0.0, -jnp.inf).astype(F32)

    def rows_of(zz, c):
        return pl.ds(pl.multiple_of((zz * 2 + c) * 96, 32), 96)

    def block(j, y, zz, c):
        return W.at[j, :, y, rows_of(zz, c), :]

    def half(j, st, y, zz, c):
        return W.at[j, st, y, rows_of(zz, c), :]

    def gather_rows(j):
        own_copies[j].wait()
        for d in range(1, SEQ):
            src = lax.rem(S + SEQ - d, SEQ)
            arrived(slot(j, src), a2a_s.at[j, d - 1], a2a_r.at[j, d - 1], peers[d - 1])
        for st in range(2):
            rows = jnp.concatenate([A[j, st, q] for q in range(3)], axis=1)
            W[j, st, yh, rows_of(z, core), :] = jnp.dot(sel[...], rows, preferred_element_type=F32).astype(BF16)

    yy = [yh, 1 - yh]

    def sib_send(j, w, k, zz):
        b = block(j, yy[w], zz, core)
        send(b, b, sib_s.at[j, w, k], sib_r.at[j, w, k], sib)

    def begin(j):
        gather_rows(j)
        b = block(j, yh, z, core)
        send(b, b, y_s.at[j], y_r.at[j], yp)
        send(b, b, zr_s.at[j, 0, 0], zr_r.at[j, 0, 0], zr)
        send(b, b, zl_s.at[j, 0, 0], zl_r.at[j, 0, 0], zl)
        sib_send(j, 0, 0, z)

    def begin_partner(j):
        b = block(j, 1 - yh, z, core)
        arrived(b, y_s.at[j], y_r.at[j], yp)
        send(b, b, zr_s.at[j, 1, 0], zr_r.at[j, 1, 0], zr)
        send(b, b, zl_s.at[j, 1, 0], zl_r.at[j, 1, 0], zl)
        sib_send(j, 1, 0, z)

    def hop(j, w, step):
        y = yy[w]
        if step < 4:
            b = block(j, y, up(-step), core)
            arrived(b, zr_s.at[j, w, step - 1], zr_r.at[j, w, step - 1], zr)
            f = b if step < 3 else half(j, 0, y, up(-step), core)
            send(f, f, zr_s.at[j, w, step], zr_r.at[j, w, step], zr)
            sib_send(j, w, step, up(-step))
            b = block(j, y, up(step), core)
            arrived(b, zl_s.at[j, w, step - 1], zl_r.at[j, w, step - 1], zl)
            f = b if step < 3 else half(j, 1, y, up(step), core)
            send(f, f, zl_s.at[j, w, step], zl_r.at[j, w, step], zl)
            sib_send(j, w, step + 3, up(step))
        else:
            arrived(half(j, 0, y, up(4), core), zr_s.at[j, w, 3], zr_r.at[j, w, 3], zr)
            arrived(half(j, 1, y, up(4), core), zl_s.at[j, w, 3], zl_r.at[j, w, 3], zl)
            sib_send(j, w, 7, up(4))

    def sib_arrived(j):
        for w in range(2):
            for k, dz in enumerate((0, -1, -2, -3, 1, 2, 3, 4)):
                arrived(block(j, yy[w], up(dz), 1 - core), sib_s.at[j, w, k], sib_r.at[j, w, k], sib)

    def project(j, st):
        n, base = (TXT, 0) if st == 0 else (IMG, TXT)
        lhs = T[:, 64 * st : 64 * st + 64, :].reshape(SEQ * 64, D)
        if st == 1:
            lhs = jnp.concatenate([lhs, XR[...]], axis=0)
        rows = jnp.dot(lhs, W[j, st].reshape(D, 3 * HD), preferred_element_type=F32)
        for part, store in ((0, Q), (1, K)):
            v = rows[:, part * HD : (part + 1) * HD]
            power = jnp.mean(v * v, axis=-1, keepdims=True)
            v = v * lax.rsqrt(power + 1e-06) * gains[2 * st + part : 2 * st + part + 1, :]
            if st == 1:
                even = lax.rem(lax.broadcasted_iota(jnp.int32, (n, HD), 1), 2) == 0
                turned = jnp.where(even, pltpu.roll(v, HD - 1, 1), pltpu.roll(v, 1, 1))
                v = v * cosine[...] + turned * sine[...]
            store[base : base + n, :] = v.astype(BF16)
        V[base : base + n, 0:HD] = rows[:, 2 * HD : 3 * HD].astype(BF16)

    def attend_rows(q):
        scores = lax.dot_general(q, K[...], (((1,), (1,)), ((), ())), preferred_element_type=F32)
        scores = jnp.concatenate([scores[:, :TXT] + bias[0:1, :], scores[:, TXT:]], axis=1)
        weight = jnp.exp2((scores - jnp.max(scores, axis=-1, keepdims=True)) * SCALE)
        mixed = jnp.dot(weight.astype(BF16), V[...], preferred_element_type=F32)
        return mixed[:, :HD] / mixed[:, HD:]

    def attend(j):
        first = attend_rows(Q[0:544, :])
        second = attend_rows(Q[544:1088, :])
        OB[j, :, 0:64, :] = first[0:512].astype(BF16).reshape(SEQ, 64, HD)
        image_rows = jnp.concatenate([first[512:544], second[0:480]], axis=0)
        OB[j, :, 64:128, :] = image_rows.astype(BF16).reshape(SEQ, 64, HD)
        rest_rows = second[480:544].reshape(SEQ, REST, HD)
        OB[j, :, 128:144, :] = jnp.concatenate([rest_rows, jnp.zeros_like(rest_rows)], axis=1).astype(BF16)

    def give(j):
        lanes = pl.ds(pl.multiple_of((S * HEADS_HERE + j) * HD, HD), HD)
        for d in range(1, SEQ):
            send(OB.at[j, peers[d - 1][1]], out.at[:, lanes], out_s.at[j, d - 1], out_r.at[j, d - 1], peers[d - 1])
        out[:, lanes] = OB[j, S]

    def take(j):
        for d in range(1, SEQ):
            src = lax.rem(S + SEQ - d, SEQ)
            lanes = pl.ds(pl.multiple_of((src * HEADS_HERE + j) * HD, HD), HD)
            arrived(out.at[:, lanes], out_s.at[j, d - 1], out_r.at[j, d - 1], peers[d - 1])

    def parts_of(j):
        return [
            lambda: (sib_arrived(j), project(j, 0)),
            lambda: project(j, 1),
            lambda: (attend(j), give(j)),
        ]

    OWN, PARTNER = 0, 1
    begin(0)
    begin_partner(0)
    begin(1)
    gather_rows(2)
    b2 = block(2, yh, z, core)
    send(b2, b2, y_s.at[2], y_r.at[2], yp)
    send_tokens(S, 0, d_xr)
    send_tokens(S, 2, d_xl)
    send_tokens(S, 4, d_yp)
    begin_partner(1)
    units = ((0, OWN), (0, PARTNER), (1, OWN), (1, PARTNER))
    for j, w in units:
        hop(j, w, 1)
    hop(0, OWN, 2)
    hop(0, PARTNER, 2)
    tokens_arrived(s_xl, 0, d_xr)
    send(T.at[s_xl, 0:64], T.at[s_xl, 0:64], tok_s.at[6], tok_r.at[6], d_xr)
    tokens_arrived(s_xr, 2, d_xl)
    send(T.at[s_xr, 64:128], T.at[s_xr, 64:128], tok_s.at[7], tok_r.at[7], d_xl)
    send(RM.at[s_xr], RM.at[s_xr], tok_s.at[8], tok_r.at[8], d_xl)
    hop(1, OWN, 2)
    hop(1, PARTNER, 2)
    tokens_arrived(s_yp, 4, d_yp)
    send_tokens(s_yp, 9, d_xr)
    send_tokens(s_yp, 11, d_xl)
    hop(0, OWN, 3)
    hop(0, PARTNER, 3)
    b2 = block(2, yh, z, core)
    send(b2, b2, zr_s.at[2, 0, 0], zr_r.at[2, 0, 0], zr)
    send(b2, b2, zl_s.at[2, 0, 0], zl_r.at[2, 0, 0], zl)
    sib_send(2, 0, 0, z)
    arrived(T.at[s_xx, 0:64], tok_s.at[6], tok_r.at[6], d_xr)
    arrived(T.at[s_xx, 64:128], tok_s.at[7], tok_r.at[7], d_xl)
    arrived(RM.at[s_xx], tok_s.at[8], tok_r.at[8], d_xl)
    send_tokens(s_xx, 13, d_yp)
    hop(1, OWN, 3)
    begin_partner(2)
    hop(1, PARTNER, 3)
    for j, w in units:
        hop(j, w, 4)
    hop(2, OWN, 1)
    hop(2, PARTNER, 1)
    tokens_arrived(o_xl, 9, d_xr)
    tokens_arrived(o_xr, 11, d_xl)
    tokens_arrived(o_xx, 13, d_yp)

    def unpack(i, carry):
        pair = [RM[2 * i + n].astype(F32) for n in range(2)]
        rows = [jnp.concatenate([p[0:8], p[8:16]], axis=1) for p in pair]
        XR[pl.ds(pl.multiple_of(i * 16, 16), 16), :] = jnp.concatenate(rows, axis=0).astype(BF16)
        return carry

    lax.fori_loop(0, 4, unpack, 0)
    V[:, HD:] = jnp.ones((TOTAL, HD), BF16)
    todo = parts_of(0) + parts_of(1)
    for step in (2, 3, 4):
        for w in (0, 1):
            todo.pop(0)()
            hop(2, w, step)
    for part in todo + parts_of(2):
        part()
    for j in range(HEADS_HERE):
        take(j)
    for copy in pending:
        copy.wait_send()


def on_device(text_tokens, image_tokens, weights, qk_gain, mod_table, text_lengths, time_index):
    mods = lax.dynamic_index_in_dim(mod_table, time_index[0], 0, keepdims=False)
    wraw = jnp.swapaxes(weights, 1, 2)
    cosine, sine = rope_rows()
    vmem = pl.BlockSpec(memory_space=pltpu.VMEM)
    dma = pltpu.SemaphoreType.DMA
    n_tok = 15
    result = pl.pallas_call(
        kernel,
        out_shape=jax.ShapeDtypeStruct((144, D), BF16),
        in_specs=[vmem] * 7 + [pl.BlockSpec(memory_space=pltpu.SMEM)],
        out_specs=vmem,
        scratch_shapes=[
            pltpu.VMEM((2, 3, 16, D), BF16),
            pltpu.VMEM((HEADS_HERE, 2, 2, D // 2, 3 * HD), BF16),
            pltpu.VMEM((HEADS_HERE, 2, 3, 128, HD), BF16),
            pltpu.VMEM((SEQ, 128, D), BF16),
            pltpu.VMEM((SEQ, 16, D // 2), BF16),
            pltpu.VMEM((SEQ * REST, D), BF16),
            pltpu.VMEM((TOTAL, HD), BF16),
            pltpu.VMEM((TOTAL, HD), BF16),
            pltpu.VMEM((TOTAL, 2 * HD), BF16),
            pltpu.VMEM((HEADS_HERE, SEQ, 144, HD), BF16),
            pltpu.VMEM((8, TXT), F32),
            pltpu.VMEM((96, 128), BF16),
            dma((3, 7)), dma((3, 7)),
            dma((3,)), dma((3,)),
            dma((3, 2, 4)), dma((3, 2, 4)),
            dma((3, 2, 4)), dma((3, 2, 4)),
            dma((3, 2, 8)), dma((3, 2, 8)),
            dma((n_tok,)), dma((n_tok,)),
            dma((3, 7)), dma((3, 7)),
            dma((3,)),
        ],
        compiler_params=pltpu.CompilerParams(
            collective_id=0, has_side_effects=True, vmem_limit_bytes=36 * 1024 * 1024
        ),
        cost_estimate=pl.CostEstimate(flops=9_500_000_000, bytes_accessed=30_000_000, transcendentals=3_600_000),
        name="joint_attention",
    )(
        wraw, text_tokens[0], image_tokens[0], mods, qk_gain.reshape(4, HD),
        jnp.asarray(cosine), jnp.asarray(sine), text_lengths.astype(jnp.int32),
    )
    return result[None, :TROWS], result[None, TROWS : TROWS + IROWS]


def solution(mesh):
    placed = (
        P("rep", "seq", None),
        P("rep", "seq", None),
        P(None, ("rep", "seq"), None, None),
        P(),
        P(),
        P("rep"),
        P("rep"),
    )
    return jax.shard_map(
        on_device,
        mesh=mesh,
        in_specs=placed,
        out_specs=(P("rep", "seq", None), P("rep", "seq", None)),
        check_vma=False,
    )
```

```python
import functools

import jax
import jax.numpy as jnp
import numpy as np
from jax import lax
from jax.experimental import pallas as pl
from jax.experimental.pallas import tpu as pltpu
from jax.sharding import PartitionSpec as P

D = 3072
HD = 128
GRID = 24
TXT = 512
IMG = GRID * GRID
TOTAL = TXT + IMG
SEQ = 8
NZ = 8
HEADS_HERE = 3
TROWS = TXT // SEQ
IROWS = IMG // SEQ
REST = IROWS - 64
WROWS = 12
KSTEP = 768
SCALE = float(HD**-0.5 * np.log2(np.e))
MESH = pl.DeviceIdType.MESH
BF16, F32 = jnp.bfloat16, jnp.float32


def rope_rows():
    pairs, still = HD // 2, HD // 16
    rows = (pairs - still) // 2
    cols = pairs - still - rows
    place = np.concatenate(
        [
            (np.arange(SEQ)[:, None] * IROWS + np.arange(64)[None, :]).reshape(-1),
            (np.arange(SEQ)[:, None] * IROWS + 64 + np.arange(REST)[None, :]).reshape(-1),
        ]
    )
    row_pos = (place // GRID).astype(np.float32)
    col_pos = (place % GRID).astype(np.float32)
    row_freq = (10000.0 ** (-np.arange(rows) / rows)).astype(np.float32)
    col_freq = (10000.0 ** (-np.arange(cols) / cols)).astype(np.float32)
    angles = np.concatenate(
        [
            np.zeros((IMG, still), np.float32),
            row_pos[:, None] * row_freq[None, :],
            col_pos[:, None] * col_freq[None, :],
        ],
        axis=1,
    )
    cosine = np.repeat(np.cos(angles), 2, axis=1)
    sine = np.repeat(np.sin(angles), 2, axis=1)
    sine[:, 0::2] *= -1.0
    return cosine.astype(np.float32), sine.astype(np.float32)


def kernel(
    wraw, text_hbm, image_hbm, mods_hbm, gains_hbm, cosine_hbm, sine_hbm, length, step_index,
    out,
    picked,     text, image, mods, gains, cosine, sine, wsrc, W, A, T, RM, XR, Q, K, V, OB, bias, sel, acc,
    a2a_s, a2a_r, y_s, y_r, zr_s, zr_r, zl_s, zl_r, sib_s, sib_r, yc_s, yc_r, sc_s, sc_r, tok_s, tok_r, out_s, out_r, own_sem, load_sem,
):
    R, S = lax.axis_index("rep"), lax.axis_index("seq")
    core = lax.rem(R, 2)
    z = lax.rem(R // 2, NZ)
    yh = R // (2 * NZ)
    x = lax.rem(S, 4)
    yl = S // 4

    def rep_of(y, zz, c):
        return (y * NZ + zz) * 2 + c

    def up(dz):
        return lax.rem(z + dz + NZ, NZ)

    def xs(dx, row):
        return row * 4 + lax.rem(x + dx + 4, 4)

    sib = (rep_of(yh, z, 1 - core), S)
    zr = (rep_of(yh, up(1), core), S)
    zl = (rep_of(yh, up(-1), core), S)
    yp = (rep_of(1 - yh, z, core), S)
    peers = [(R, lax.rem(S + d, SEQ)) for d in range(1, SEQ)]
    s_yp, s_xr, s_xl, s_xx = xs(0, 1 - yl), xs(1, yl), xs(-1, yl), xs(2, yl)
    o_xr, o_xl, o_xx = xs(1, 1 - yl), xs(-1, 1 - yl), xs(2, 1 - yl)

    loads = []
    for i, (far, near) in enumerate(
        [(mods_hbm, mods), (text_hbm, text), (image_hbm, image), (gains_hbm, gains), (cosine_hbm, cosine), (sine_hbm, sine)]
    ):
        loads.append(pltpu.make_async_copy(far, near, load_sem.at[i]))
        loads[-1].start()

    wsrc[:, :, 0:WROWS, :] = wraw[...]
    wsrc[:, :, WROWS:16, :] = jnp.zeros((2, 3, 16 - WROWS, D), BF16)

    barrier = pltpu.get_barrier_semaphore()
    partners = [sib, zr, zl, yp] + peers
    for device in partners:
        pl.semaphore_signal(barrier, inc=1, device_id=device, device_id_type=MESH)
    pl.semaphore_wait(barrier, len(partners))

    pending = []

    def send(src, dst, ssem, rsem, device):
        copy = pltpu.make_async_remote_copy(
            src_ref=src, dst_ref=dst, send_sem=ssem, recv_sem=rsem, device_id=device, device_id_type=MESH
        )
        copy.start()
        pending.append(copy)

    def arrived(dst, ssem, rsem, device):
        pltpu.make_async_remote_copy(
            src_ref=dst, dst_ref=dst, send_sem=ssem, recv_sem=rsem, device_id=device, device_id_type=MESH
        ).wait_recv()

    def slot(j, s):
        return A.at[j, :, :, pl.ds(pl.multiple_of(s * 16, 16), 16), :]

    def piece(j, g):
        return wsrc.at[:, :, :, pl.ds(pl.multiple_of(g * (HEADS_HERE * HD) + j * HD, HD), HD)]

    def a2a_start(j):
        for d in range(1, SEQ):
            send(piece(j, peers[d - 1][1]), slot(j, S), a2a_s.at[j, d - 1], a2a_r.at[j, d - 1], peers[d - 1])
        copy = pltpu.make_async_copy(piece(j, S), slot(j, S), own_sem.at[j])
        copy.start()
        return copy

    own_copies = [a2a_start(0)]

    i96 = lax.broadcasted_iota(jnp.int32, (96, 128), 0)
    i128 = lax.broadcasted_iota(jnp.int32, (96, 128), 1)
    sel[...] = jnp.where(i128 == (i96 // WROWS) * 16 + lax.rem(i96, WROWS), 1.0, 0.0).astype(BF16)

    for copy in loads[:3]:
        copy.wait()
    for stream in range(2):
        row = jnp.zeros((2, D), F32)
        for i in range(mods.shape[0]):
            row = row + jnp.where(step_index[...] == i, mods[i, stream], 0.0)
        picked[stream] = row

    def modulate(rows, stream):
        v = rows.astype(F32)
        center = v - jnp.mean(v, axis=-1, keepdims=True)
        spread = jnp.mean(center * center, axis=-1, keepdims=True)
        normed = center * lax.rsqrt(spread + 1e-06)
        return normed * (1.0 + picked[stream, 1:2, :]) + picked[stream, 0:1, :]

    def mod_text(i, carry):
        rows = pl.ds(pl.multiple_of(i * 16, 16), 16)
        T[S, rows, :] = modulate(text[rows, :], 0).astype(BF16)
        return carry

    def mod_image(i, carry):
        rows = pl.ds(pl.multiple_of(i * 16, 16), 16)
        T[S, pl.ds(pl.multiple_of(64 + i * 16, 16), 16), :] = modulate(image[rows, :], 1).astype(BF16)
        return carry

    lax.fori_loop(0, 4, mod_text, 0)
    lax.fori_loop(0, 4, mod_image, 0)
    rest = modulate(image[64:72, :], 1)
    RM[S] = jnp.concatenate([rest[:, : D // 2], rest[:, D // 2 :]], axis=0).astype(BF16)

    def send_tokens(s, first, device):
        send(T.at[s], T.at[s], tok_s.at[first], tok_r.at[first], device)
        send(RM.at[s], RM.at[s], tok_s.at[first + 1], tok_r.at[first + 1], device)

    def tokens_arrived(s, first, device):
        arrived(T.at[s], tok_s.at[first], tok_r.at[first], device)
        arrived(RM.at[s], tok_s.at[first + 1], tok_r.at[first + 1], device)

    own_copies.append(a2a_start(1))
    d_yp, d_xr, d_xl = (R, s_yp), (R, s_xr), (R, s_xl)
    def rows_of(zz, c):
        return pl.ds(pl.multiple_of((zz * 2 + c) * 96, 32), 96)

    def block(j, y, zz, c):
        return W.at[j, :, y, rows_of(zz, c), :]

    def half(j, st, y, zz, c):
        return W.at[j, st, y, rows_of(zz, c), :]

    def gather_rows(j):
        own_copies[j].wait()
        for d in range(1, SEQ):
            src = lax.rem(S + SEQ - d, SEQ)
            arrived(slot(j, src), a2a_s.at[j, d - 1], a2a_r.at[j, d - 1], peers[d - 1])
        for st in range(2):
            rows = jnp.concatenate([A[j, st, q] for q in range(3)], axis=1)
            W[j, st, yh, rows_of(z, core), :] = jnp.dot(sel[...], rows, preferred_element_type=F32).astype(BF16)

    yy = [yh, 1 - yh]

    def split(j, w):
        return (j, w) == (2, 1)

    def ring_block(j, w, zz):
        return half(j, 0, yy[w], zz, core) if split(j, w) else block(j, yy[w], zz, core)

    def sib_send(j, w, k, zz):
        b = ring_block(j, w, zz) if k else block(j, yy[w], zz, core)
        send(b, b, sib_s.at[j, w, k], sib_r.at[j, w, k], sib)

    def first(j, w):
        b = ring_block(j, w, z)
        send(b, b, zr_s.at[j, w, 0], zr_r.at[j, w, 0], zr)
        send(b, b, zl_s.at[j, w, 0], zl_r.at[j, w, 0], zl)
        sib_send(j, w, 0, z)

    def collect(j):
        gather_rows(j)
        b = block(j, yh, z, core)
        send(b, b, y_s.at[j], y_r.at[j], yp)

    def partner_rows(j):
        arrived(block(j, 1 - yh, z, core), y_s.at[j], y_r.at[j], yp)

    def cross(j, w, k, zz):
        if split(j, 1) and w == 0:
            b = half(j, 1, yh, zz, core)
            send(b, b, yc_s.at[k - 1], yc_r.at[k - 1], yp)

    def cross_arrived(j, ks):
        if not split(j, 1):
            return
        for k, dz in ((1, -1), (2, -2), (3, -3), (4, 1), (5, 2), (6, 3), (7, 4)):
            if k not in ks:
                continue
            b = half(j, 1, 1 - yh, up(dz), core)
            arrived(b, yc_s.at[k - 1], yc_r.at[k - 1], yp)
            send(b, b, sc_s.at[k - 1], sc_r.at[k - 1], sib)

    def hop(j, w, step):
        if step < 4:
            for sems, sign, k in (((zr_s, zr_r, zr), -1, step), ((zl_s, zl_r, zl), 1, step + 3)):
                b = ring_block(j, w, up(sign * step))
                arrived(b, sems[0].at[j, w, step - 1], sems[1].at[j, w, step - 1], sems[2])
                f = b if step < 3 else half(j, 0 if sign < 0 else 1, yy[w], up(sign * step), core)
                if step < 3 or sign < 0 or not split(j, w):
                    send(f, f, sems[0].at[j, w, step], sems[1].at[j, w, step], sems[2])
                sib_send(j, w, k, up(sign * step))
                cross(j, w, k, up(sign * step))
        else:
            arrived(half(j, 0, yy[w], up(4), core), zr_s.at[j, w, 3], zr_r.at[j, w, 3], zr)
            if not split(j, w):
                arrived(half(j, 1, yy[w], up(4), core), zl_s.at[j, w, 3], zl_r.at[j, w, 3], zl)
            sib_send(j, w, 7, up(4))
            cross(j, w, 7, up(4))

    def sib_arrived(j, ks=range(8)):
        for w in range(2):
            for k, dz in enumerate((0, -1, -2, -3, 1, 2, 3, 4)):
                if k not in ks:
                    continue
                whole = block(j, yy[w], up(dz), 1 - core)
                b = half(j, 0, yy[w], up(dz), 1 - core) if k and split(j, w) else whole
                arrived(b, sib_s.at[j, w, k], sib_r.at[j, w, k], sib)
                if k and split(j, w):
                    b = half(j, 1, yy[w], up(dz), 1 - core)
                    arrived(b, sc_s.at[k - 1], sc_r.at[k - 1], sib)

    def prepare(j, st, rows, places, start):
        def table(ref):
            return jnp.concatenate([ref[pl.ds(at - start, n), :] for at, n in places], axis=0)

        for part, store in ((0, Q), (1, K), (2, V)):
            v = rows[:, part * HD : (part + 1) * HD]
            if part < 2:
                power = jnp.mean(v * v, axis=-1, keepdims=True)
                v = v * lax.rsqrt(power + 1e-06) * gains[2 * st + part : 2 * st + part + 1, :]
                if st == 1:
                    even = lax.rem(lax.broadcasted_iota(jnp.int32, v.shape, 1), 2) == 0
                    turned = jnp.where(even, pltpu.roll(v, HD - 1, 1), pltpu.roll(v, 1, 1))
                    v = v * table(cosine) + turned * table(sine)
            v = v.astype(BF16)
            done = 0
            for at, n in places:
                store[j, pl.ds(at, n), 0:HD] = v[done : done + n]
                done += n

    near, distant = (S, s_xl, s_xr, s_yp, s_xx), (o_xl, o_xr, o_xx)

    def project(j, st, slots):
        base = TXT * st
        lhs = [T[s, 64 * st : 64 * st + 64, :] for s in slots]
        places = [(pl.multiple_of(base + s * 64, 64), 64) for s in slots]
        if st == 1 and slots is distant:
            lhs.append(XR[...])
            places.append((TXT + 512, 64))
        rows = jnp.dot(
            jnp.concatenate(lhs, axis=0), W[j, st].reshape(D, 3 * HD), preferred_element_type=F32
        )
        prepare(j, st, rows, places, TXT)

    def partial(j, st, quarters):
        total = None
        for q in quarters:
            cols = [pl.ds(pl.multiple_of(y * (D // 2) + q * 384, 128), 384) for y in range(2)]
            lhs = jnp.concatenate(
                [T[:, 64 * st : 64 * st + 64, c].reshape(SEQ * 64, 384) for c in cols], axis=1
            )
            if st == 1:
                lhs = jnp.concatenate([lhs, jnp.concatenate([XR[:, c] for c in cols], axis=1)], axis=0)
            rhs = jnp.concatenate([W[j, st, y, pl.ds(pl.multiple_of(q * 384, 128), 384), :] for y in range(2)], axis=0)
            term = jnp.dot(lhs, rhs, preferred_element_type=F32)
            total = term if total is None else total + term
        return total

    quarter = z // 2

    def project_some(j, st, quarters):
        at, n = ((0, TXT), (TXT, IMG))[st]
        total = partial(j, st, quarters)
        acc[at : at + n, :] = total if len(quarters) == 2 else acc[at : at + n, :] + total

    side = 2 * lax.rem(z, 2) - 1
    order = [quarter, lax.rem(quarter + side + 4, 4), lax.rem(quarter - side + 4, 4), lax.rem(quarter + 2, 4)]

    def project_last(j):
        for st, at, n in ((0, 0, TXT), (1, TXT, IMG)):
            rows = acc[at : at + n, :] + partial(j, st, order[3:])
            prepare(j, st, rows, [(at, n)], TXT)

    def attend_rows(j, q):
        scores = lax.dot_general(q, K[j], (((1,), (1,)), ((), ())), preferred_element_type=F32)
        scores = jnp.concatenate([scores[:, :TXT] + bias[0:1, :], scores[:, TXT:]], axis=1)
        weight = jnp.exp2((scores - jnp.max(scores, axis=-1, keepdims=True)) * SCALE)
        mixed = jnp.dot(weight.astype(BF16), V[j], preferred_element_type=F32)
        return mixed[:, :HD] / mixed[:, HD:]

    def attend(j):
        first = attend_rows(j, Q[j, 0:544, :])
        second = attend_rows(j, Q[j, 544:1088, :])
        OB[j, :, 0:64, :] = first[0:512].astype(BF16).reshape(SEQ, 64, HD)
        image_rows = jnp.concatenate([first[512:544], second[0:480]], axis=0)
        OB[j, :, 64:128, :] = image_rows.astype(BF16).reshape(SEQ, 64, HD)
        rest_rows = second[480:544].reshape(SEQ, REST, HD)
        OB[j, :, 128:144, :] = jnp.concatenate([rest_rows, jnp.zeros_like(rest_rows)], axis=1).astype(BF16)

    def give(j):
        lanes = pl.ds(pl.multiple_of((S * HEADS_HERE + j) * HD, HD), HD)
        for d in range(1, SEQ):
            send(OB.at[j, peers[d - 1][1]], out.at[:, lanes], out_s.at[j, d - 1], out_r.at[j, d - 1], peers[d - 1])
        out[:, lanes] = OB[j, S]

    def take(j):
        for d in range(1, SEQ):
            src = lax.rem(S + SEQ - d, SEQ)
            lanes = pl.ds(pl.multiple_of((src * HEADS_HERE + j) * HD, HD), HD)
            arrived(out.at[:, lanes], out_s.at[j, d - 1], out_r.at[j, d - 1], peers[d - 1])

    def unpack(i, carry):
        pair = [RM[2 * i + n].astype(F32) for n in range(2)]
        rows = [jnp.concatenate([p[0:8], p[8:16]], axis=1) for p in pair]
        XR[pl.ds(pl.multiple_of(i * 16, 16), 16), :] = jnp.concatenate(rows, axis=0).astype(BF16)
        return carry

    def text_half(s):
        return T.at[s, 0:64]

    def image_half(s):
        return T.at[s, 64:128]

    def pass_on(parts, start, device):
        for i, part in enumerate(parts):
            send(part, part, tok_s.at[start + i], tok_r.at[start + i], device)

    def came(parts, start, device):
        for i, part in enumerate(parts):
            arrived(part, tok_s.at[start + i], tok_r.at[start + i], device)

    def near_came():
        tokens_arrived(s_xl, 0, d_xr)
        pass_on([text_half(s_xl)], 6, d_xr)
        tokens_arrived(s_xr, 2, d_xl)
        pass_on([image_half(s_xr), RM.at[s_xr]], 7, d_xl)

    def partner_came():
        tokens_arrived(s_yp, 4, d_yp)
        pass_on([T.at[s_yp], RM.at[s_yp]], 9, d_xr)
        pass_on([T.at[s_yp], RM.at[s_yp]], 11, d_xl)

    def opposite_came():
        came([text_half(s_xx)], 6, d_xr)
        came([image_half(s_xx), RM.at[s_xx]], 7, d_xl)
        pass_on([T.at[s_xx], RM.at[s_xx]], 13, d_yp)

    def all_came():
        tokens_arrived(o_xl, 9, d_xr)
        tokens_arrived(o_xr, 11, d_xl)
        tokens_arrived(o_xx, 13, d_yp)
        lax.fori_loop(0, 4, unpack, 0)

    OWN, PARTNER = 0, 1

    def hops(j, step):
        hop(j, OWN, step)
        hop(j, PARTNER, step)

    collect(0)
    first(0, OWN)
    where = lax.broadcasted_iota(jnp.int32, (8, TXT), 1)
    bias[...] = jnp.where(where < length[...], 0.0, -jnp.inf).astype(F32)
    collect(1)
    first(1, OWN)
    send_tokens(S, 0, d_xr)
    send_tokens(S, 2, d_xl)
    partner_rows(0)
    first(0, PARTNER)
    partner_rows(1)
    first(1, PARTNER)
    send_tokens(S, 4, d_yp)
    own_copies.append(a2a_start(2))
    V[:, :, HD:] = jnp.ones((HEADS_HERE, TOTAL, HD), BF16)
    hops(0, 1)
    hops(1, 1)
    hops(0, 2)
    near_came()
    hops(1, 2)
    collect(2)
    partner_came()
    hops(0, 3)
    first(2, OWN)
    opposite_came()
    hop(1, OWN, 3)
    partner_rows(2)
    first(2, PARTNER)
    hop(1, PARTNER, 3)
    hops(0, 4)
    hop(2, OWN, 1)
    hop(1, OWN, 4)
    hop(2, PARTNER, 1)
    hop(1, PARTNER, 4)
    for copy in loads[3:]:
        copy.wait()
    sib_arrived(0)
    project(0, 0, near)
    project(0, 1, near)
    sib_arrived(1)
    project(1, 0, near)
    project(1, 1, near)
    hop(2, OWN, 2)
    all_came()
    project(0, 0, distant)
    hop(2, PARTNER, 2)
    project(0, 1, distant)
    attend(0)
    hop(2, OWN, 3)
    give(0)
    hop(2, PARTNER, 3)
    project(1, 0, distant)
    project(1, 1, distant)
    cross_arrived(2, (1, 2, 4, 5))
    sib_arrived(2, (0, 1, 2, 4, 5))
    project_some(2, 0, order[0:2])
    hop(2, OWN, 4)
    hop(2, PARTNER, 4)
    project_some(2, 1, order[0:2])
    attend(1)
    give(1)
    cross_arrived(2, (3, 6, 7))
    sib_arrived(2, (3, 6))
    project_some(2, 0, order[2:3])
    project_some(2, 1, order[2:3])
    sib_arrived(2, (7,))
    project_last(2)
    attend(2)
    give(2)
    for j in range(HEADS_HERE):
        take(j)
    for copy in pending:
        copy.wait_send()


def cut(rows, text, image):
    text[0] = rows[0:TROWS, :]
    image[0] = rows[TROWS : TROWS + IROWS, :]


def on_device(text_tokens, image_tokens, weights, qk_gain, mod_table, text_lengths, time_index):
    wraw = jnp.swapaxes(weights, 1, 2)
    cosine, sine = rope_rows()
    vmem = pl.BlockSpec(memory_space=pltpu.VMEM)
    dma = pltpu.SemaphoreType.DMA
    n_tok = 15
    result = pl.pallas_call(
        kernel,
        out_shape=jax.ShapeDtypeStruct((144, D), BF16),
        in_specs=[vmem] + [pl.BlockSpec(memory_space=pltpu.HBM)] * 6 + [vmem] * 2,
        out_specs=vmem,
        scratch_shapes=[
            pltpu.VMEM((2, 2, D), F32),
            pltpu.VMEM(text_tokens.shape[1:], BF16),
            pltpu.VMEM(image_tokens.shape[1:], BF16),
            pltpu.VMEM(mod_table.shape, F32),
            pltpu.VMEM((4, HD), F32),
            pltpu.VMEM((IMG, HD), F32),
            pltpu.VMEM((IMG, HD), F32),
            pltpu.VMEM((2, 3, 16, D), BF16),
            pltpu.VMEM((HEADS_HERE, 2, 2, D // 2, 3 * HD), BF16),
            pltpu.VMEM((HEADS_HERE, 2, 3, 128, HD), BF16),
            pltpu.VMEM((SEQ, 128, D), BF16),
            pltpu.VMEM((SEQ, 16, D // 2), BF16),
            pltpu.VMEM((SEQ * REST, D), BF16),
            pltpu.VMEM((HEADS_HERE, TOTAL, HD), BF16),
            pltpu.VMEM((HEADS_HERE, TOTAL, HD), BF16),
            pltpu.VMEM((HEADS_HERE, TOTAL, 2 * HD), BF16),
            pltpu.VMEM((HEADS_HERE, SEQ, 144, HD), BF16),
            pltpu.VMEM((8, TXT), F32),
            pltpu.VMEM((96, 128), BF16),
            pltpu.VMEM((TOTAL, 3 * HD), F32),
            dma((3, 7)), dma((3, 7)),
            dma((3,)), dma((3,)),
            dma((3, 2, 4)), dma((3, 2, 4)),
            dma((3, 2, 4)), dma((3, 2, 4)),
            dma((3, 2, 8)), dma((3, 2, 8)),
            dma((7,)), dma((7,)),
            dma((7,)), dma((7,)),
            dma((n_tok,)), dma((n_tok,)),
            dma((3, 7)), dma((3, 7)),
            dma((3,)),
            dma((6,)),
        ],
        compiler_params=pltpu.CompilerParams(
            collective_id=0, has_side_effects=True, vmem_limit_bytes=56 * 1024 * 1024
        ),
        cost_estimate=pl.CostEstimate(flops=9_500_000_000, bytes_accessed=30_000_000, transcendentals=3_600_000),
        name="joint_attention",
    )(
        wraw, text_tokens[0], image_tokens[0], mod_table, qk_gain.reshape(4, HD),
        jnp.asarray(cosine), jnp.asarray(sine), text_lengths.astype(jnp.int32).reshape(1, 1),
        time_index.astype(jnp.int32).reshape(1, 1),
    )
    return pl.pallas_call(
        cut,
        out_shape=(
            jax.ShapeDtypeStruct((1, TROWS, D), BF16),
            jax.ShapeDtypeStruct((1, IROWS, D), BF16),
        ),
        in_specs=[vmem],
        out_specs=(vmem, vmem),
        name="cut_outputs",
    )(result)


def solution(mesh):
    placed = (
        P("rep", "seq", None),
        P("rep", "seq", None),
        P(None, ("rep", "seq"), None, None),
        P(),
        P(),
        P("rep"),
        P("rep"),
    )
    return jax.shard_map(
        on_device,
        mesh=mesh,
        in_specs=placed,
        out_specs=(P("rep", "seq", None), P("rep", "seq", None)),
        check_vma=False,
    )
```

```python
import functools

import jax
import jax.numpy as jnp
import numpy as np
from jax import lax
from jax.experimental import pallas as pl
from jax.experimental.pallas import tpu as pltpu
from jax.sharding import PartitionSpec as P

D = 3072
HD = 128
GRID = 24
TXT = 512
IMG = GRID * GRID
TOTAL = TXT + IMG
SEQ = 8
NZ = 8
HEADS_HERE = 3
TROWS = TXT // SEQ
IROWS = IMG // SEQ
REST = IROWS - 64
WROWS = 12
KSTEP = 768
SCALE = float(HD**-0.5 * np.log2(np.e))
MESH = pl.DeviceIdType.MESH
BF16, F32 = jnp.bfloat16, jnp.float32


def rope_rows():
    pairs, still = HD // 2, HD // 16
    rows = (pairs - still) // 2
    cols = pairs - still - rows
    place = np.concatenate(
        [
            (np.arange(SEQ)[:, None] * IROWS + np.arange(64)[None, :]).reshape(-1),
            (np.arange(SEQ)[:, None] * IROWS + 64 + np.arange(REST)[None, :]).reshape(-1),
        ]
    )
    row_pos = (place // GRID).astype(np.float32)
    col_pos = (place % GRID).astype(np.float32)
    row_freq = (10000.0 ** (-np.arange(rows) / rows)).astype(np.float32)
    col_freq = (10000.0 ** (-np.arange(cols) / cols)).astype(np.float32)
    angles = np.concatenate(
        [
            np.zeros((IMG, still), np.float32),
            row_pos[:, None] * row_freq[None, :],
            col_pos[:, None] * col_freq[None, :],
        ],
        axis=1,
    )
    cosine = np.repeat(np.cos(angles), 2, axis=1)
    sine = np.repeat(np.sin(angles), 2, axis=1)
    sine[:, 0::2] *= -1.0
    return cosine.astype(np.float32), sine.astype(np.float32)


def kernel(
    wraw_hbm, text_hbm, image_hbm, mods_hbm, gains_hbm, cosine_hbm, sine_hbm, length, step_index,
    out,
    wraw, picked, text, image, mods, gains, cosine, sine, wsrc, W, A, T, RM, XR, Q, K, V, OB, bias, sel, acc,
    a2a_s, a2a_r, y_s, y_r, zr_s, zr_r, zl_s, zl_r, sib_s, sib_r, yc_s, yc_r, sc_s, sc_r, tok_s, tok_r, out_s, out_r, own_sem, load_sem,
):
    R, S = lax.axis_index("rep"), lax.axis_index("seq")
    core = lax.rem(R, 2)
    z = lax.rem(R // 2, NZ)
    yh = R // (2 * NZ)
    x = lax.rem(S, 4)
    yl = S // 4

    def rep_of(y, zz, c):
        return (y * NZ + zz) * 2 + c

    def up(dz):
        return lax.rem(z + dz + NZ, NZ)

    def xs(dx, row):
        return row * 4 + lax.rem(x + dx + 4, 4)

    sib = (rep_of(yh, z, 1 - core), S)
    zr = (rep_of(yh, up(1), core), S)
    zl = (rep_of(yh, up(-1), core), S)
    yp = (rep_of(1 - yh, z, core), S)
    peers = [(R, lax.rem(S + d, SEQ)) for d in range(1, SEQ)]
    s_yp, s_xr, s_xl, s_xx = xs(0, 1 - yl), xs(1, yl), xs(-1, yl), xs(2, yl)
    o_xr, o_xl, o_xx = xs(1, 1 - yl), xs(-1, 1 - yl), xs(2, 1 - yl)

    barrier = pltpu.get_barrier_semaphore()
    partners = [sib, zr, zl, yp] + peers
    for device in partners:
        pl.semaphore_signal(barrier, inc=1, device_id=device, device_id_type=MESH)
    loads = []
    for i, (far, near) in enumerate(
        [(wraw_hbm, wraw), (mods_hbm, mods), (text_hbm, text), (image_hbm, image), (gains_hbm, gains), (cosine_hbm, cosine), (sine_hbm, sine)]
    ):
        loads.append(pltpu.make_async_copy(far, near, load_sem.at[i]))
        loads[-1].start()

    loads[0].wait()
    for q in range(3):
        rows = wraw[:, q].astype(F32)
        for st in range(2):
            wsrc[st, q, 0:WROWS, :] = rows[:, st, :].astype(BF16)
    wsrc[:, :, WROWS:16, :] = jnp.zeros((2, 3, 16 - WROWS, D), BF16)

    pl.semaphore_wait(barrier, len(partners))

    pending = []

    def send(src, dst, ssem, rsem, device):
        copy = pltpu.make_async_remote_copy(
            src_ref=src, dst_ref=dst, send_sem=ssem, recv_sem=rsem, device_id=device, device_id_type=MESH
        )
        copy.start()
        pending.append(copy)

    def flush(keep):
        while len(pending) > keep:
            pending.pop(0).wait_send()

    def arrived(dst, ssem, rsem, device):
        pltpu.make_async_remote_copy(
            src_ref=dst, dst_ref=dst, send_sem=ssem, recv_sem=rsem, device_id=device, device_id_type=MESH
        ).wait_recv()

    def slot(j, s):
        return A.at[j, :, :, pl.ds(pl.multiple_of(s * 16, 16), 16), :]

    def piece(j, g):
        return wsrc.at[:, :, :, pl.ds(pl.multiple_of(g * (HEADS_HERE * HD) + j * HD, HD), HD)]

    def a2a_start(j):
        for d in range(1, SEQ):
            send(piece(j, peers[d - 1][1]), slot(j, S), a2a_s.at[j, d - 1], a2a_r.at[j, d - 1], peers[d - 1])
        copy = pltpu.make_async_copy(piece(j, S), slot(j, S), own_sem.at[j])
        copy.start()
        return copy

    own_copies = [a2a_start(0), a2a_start(1)]

    i96 = lax.broadcasted_iota(jnp.int32, (96, 128), 0)
    i128 = lax.broadcasted_iota(jnp.int32, (96, 128), 1)
    sel[...] = jnp.where(i128 == (i96 // WROWS) * 16 + lax.rem(i96, WROWS), 1.0, 0.0).astype(BF16)

    def modulate(rows, stream):
        v = rows.astype(F32)
        center = v - jnp.mean(v, axis=-1, keepdims=True)
        spread = jnp.mean(center * center, axis=-1, keepdims=True)
        normed = center * lax.rsqrt(spread + 1e-06)
        return normed * (1.0 + picked[stream, 1:2, :]) + picked[stream, 0:1, :]

    def mod_text(i, carry):
        rows = pl.ds(pl.multiple_of(i * 16, 16), 16)
        T[S, rows, :] = modulate(text[rows, :], 0).astype(BF16)
        return carry

    def mod_image(i, carry):
        rows = pl.ds(pl.multiple_of(i * 16, 16), 16)
        T[S, pl.ds(pl.multiple_of(64 + i * 16, 16), 16), :] = modulate(image[rows, :], 1).astype(BF16)
        return carry

    def send_tokens(s, first, device):
        send(T.at[s], T.at[s], tok_s.at[first], tok_r.at[first], device)
        send(RM.at[s], RM.at[s], tok_s.at[first + 1], tok_r.at[first + 1], device)

    def tokens_arrived(s, first, device):
        arrived(T.at[s], tok_s.at[first], tok_r.at[first], device)
        arrived(RM.at[s], tok_s.at[first + 1], tok_r.at[first + 1], device)

    d_yp, d_xr, d_xl = (R, s_yp), (R, s_xr), (R, s_xl)
    def rows_of(zz, c):
        return pl.ds(pl.multiple_of((zz * 2 + c) * 96, 32), 96)

    def block(j, y, zz, c):
        return W.at[j, :, y, rows_of(zz, c), :]

    def half(j, st, y, zz, c):
        return W.at[j, st, y, rows_of(zz, c), :]

    def gather_rows(j):
        own_copies[j].wait()
        for d in range(1, SEQ):
            src = lax.rem(S + SEQ - d, SEQ)
            arrived(slot(j, src), a2a_s.at[j, d - 1], a2a_r.at[j, d - 1], peers[d - 1])
        for st in range(2):
            rows = jnp.concatenate([A[j, st, q] for q in range(3)], axis=1)
            W[j, st, yh, rows_of(z, core), :] = jnp.dot(sel[...], rows, preferred_element_type=F32).astype(BF16)

    yy = [yh, 1 - yh]

    def split(j, w):
        return (j, w) == (2, 1)

    def ring_block(j, w, zz):
        return half(j, 0, yy[w], zz, core) if split(j, w) else block(j, yy[w], zz, core)

    def sib_send(j, w, k, zz):
        b = ring_block(j, w, zz) if k else block(j, yy[w], zz, core)
        send(b, b, sib_s.at[j, w, k], sib_r.at[j, w, k], sib)

    def first(j, w):
        b = ring_block(j, w, z)
        send(b, b, zr_s.at[j, w, 0], zr_r.at[j, w, 0], zr)
        send(b, b, zl_s.at[j, w, 0], zl_r.at[j, w, 0], zl)
        sib_send(j, w, 0, z)

    def collect(j):
        gather_rows(j)
        b = block(j, yh, z, core)
        send(b, b, y_s.at[j], y_r.at[j], yp)

    def partner_rows(j):
        arrived(block(j, 1 - yh, z, core), y_s.at[j], y_r.at[j], yp)

    def cross(j, w, k, zz):
        if split(j, 1) and w == 0:
            b = half(j, 1, yh, zz, core)
            send(b, b, yc_s.at[k - 1], yc_r.at[k - 1], yp)

    def cross_arrived(j, ks):
        if not split(j, 1):
            return
        for k, dz in ((1, -1), (2, -2), (3, -3), (4, 1), (5, 2), (6, 3), (7, 4)):
            if k not in ks:
                continue
            b = half(j, 1, 1 - yh, up(dz), core)
            arrived(b, yc_s.at[k - 1], yc_r.at[k - 1], yp)
            send(b, b, sc_s.at[k - 1], sc_r.at[k - 1], sib)

    def hop(j, w, step):
        if step < 4:
            for sems, sign, k in (((zr_s, zr_r, zr), -1, step), ((zl_s, zl_r, zl), 1, step + 3)):
                b = ring_block(j, w, up(sign * step))
                arrived(b, sems[0].at[j, w, step - 1], sems[1].at[j, w, step - 1], sems[2])
                f = b if step < 3 else half(j, 0 if sign < 0 else 1, yy[w], up(sign * step), core)
                if step < 3 or sign < 0 or not split(j, w):
                    send(f, f, sems[0].at[j, w, step], sems[1].at[j, w, step], sems[2])
                sib_send(j, w, k, up(sign * step))
                cross(j, w, k, up(sign * step))
        else:
            arrived(half(j, 0, yy[w], up(4), core), zr_s.at[j, w, 3], zr_r.at[j, w, 3], zr)
            if not split(j, w):
                arrived(half(j, 1, yy[w], up(4), core), zl_s.at[j, w, 3], zl_r.at[j, w, 3], zl)
            sib_send(j, w, 7, up(4))
            cross(j, w, 7, up(4))

    def sib_arrived(j, ks=range(8)):
        for w in range(2):
            for k, dz in enumerate((0, -1, -2, -3, 1, 2, 3, 4)):
                if k not in ks:
                    continue
                whole = block(j, yy[w], up(dz), 1 - core)
                b = half(j, 0, yy[w], up(dz), 1 - core) if k and split(j, w) else whole
                arrived(b, sib_s.at[j, w, k], sib_r.at[j, w, k], sib)
                if k and split(j, w):
                    b = half(j, 1, yy[w], up(dz), 1 - core)
                    arrived(b, sc_s.at[k - 1], sc_r.at[k - 1], sib)

    def prepare(j, st, rows, places, start):
        def table(ref):
            return jnp.concatenate([ref[pl.ds(at - start, n), :] for at, n in places], axis=0)

        for part, store in ((0, Q), (1, K), (2, V)):
            v = rows[:, part * HD : (part + 1) * HD]
            if part < 2:
                power = jnp.mean(v * v, axis=-1, keepdims=True)
                v = v * lax.rsqrt(power + 1e-06) * gains[2 * st + part : 2 * st + part + 1, :]
                if st == 1:
                    even = lax.rem(lax.broadcasted_iota(jnp.int32, v.shape, 1), 2) == 0
                    turned = jnp.where(even, pltpu.roll(v, HD - 1, 1), pltpu.roll(v, 1, 1))
                    v = v * table(cosine) + turned * table(sine)
            v = v.astype(BF16)
            done = 0
            for at, n in places:
                store[j, pl.ds(at, n), 0:HD] = v[done : done + n]
                done += n

    near, distant = (S, s_xl, s_xr, s_yp, s_xx), (o_xl, o_xr, o_xx)

    def project(j, st, slots):
        base = TXT * st
        lhs = [T[s, 64 * st : 64 * st + 64, :] for s in slots]
        places = [(pl.multiple_of(base + s * 64, 64), 64) for s in slots]
        if st == 1 and slots is distant:
            lhs.append(XR[...])
            places.append((TXT + 512, 64))
        rows = jnp.dot(
            jnp.concatenate(lhs, axis=0), W[j, st].reshape(D, 3 * HD), preferred_element_type=F32
        )
        prepare(j, st, rows, places, TXT)

    def partial(j, st, quarters):
        total = None
        for q in quarters:
            cols = [pl.ds(pl.multiple_of(y * (D // 2) + q * 384, 128), 384) for y in range(2)]
            lhs = jnp.concatenate(
                [T[:, 64 * st : 64 * st + 64, c].reshape(SEQ * 64, 384) for c in cols], axis=1
            )
            if st == 1:
                lhs = jnp.concatenate([lhs, jnp.concatenate([XR[:, c] for c in cols], axis=1)], axis=0)
            rhs = jnp.concatenate([W[j, st, y, pl.ds(pl.multiple_of(q * 384, 128), 384), :] for y in range(2)], axis=0)
            term = jnp.dot(lhs, rhs, preferred_element_type=F32)
            total = term if total is None else total + term
        return total

    quarter = z // 2

    def project_some(j, st, quarters):
        at, n = ((0, TXT), (TXT, IMG))[st]
        total = partial(j, st, quarters)
        acc[at : at + n, :] = total if len(quarters) == 2 else acc[at : at + n, :] + total

    side = 2 * lax.rem(z, 2) - 1
    order = [quarter, lax.rem(quarter + side + 4, 4), lax.rem(quarter - side + 4, 4), lax.rem(quarter + 2, 4)]

    def project_last(j):
        for st, at, n in ((0, 0, TXT), (1, TXT, IMG)):
            rows = acc[at : at + n, :] + partial(j, st, order[3:])
            prepare(j, st, rows, [(at, n)], TXT)

    def attend_rows(j, q):
        scores = lax.dot_general(q, K[j], (((1,), (1,)), ((), ())), preferred_element_type=F32)
        scores = jnp.concatenate([scores[:, :TXT] + bias[0:1, :], scores[:, TXT:]], axis=1)
        weight = jnp.exp2((scores - jnp.max(scores, axis=-1, keepdims=True)) * SCALE)
        mixed = jnp.dot(weight.astype(BF16), V[j], preferred_element_type=F32)
        return mixed[:, :HD] / mixed[:, HD:]

    def attend(j):
        first = attend_rows(j, Q[j, 0:544, :])
        second = attend_rows(j, Q[j, 544:1088, :])
        OB[j, :, 0:64, :] = first[0:512].astype(BF16).reshape(SEQ, 64, HD)
        image_rows = jnp.concatenate([first[512:544], second[0:480]], axis=0)
        OB[j, :, 64:128, :] = image_rows.astype(BF16).reshape(SEQ, 64, HD)
        rest_rows = second[480:544].reshape(SEQ, REST, HD)
        OB[j, :, 128:144, :] = jnp.concatenate([rest_rows, jnp.zeros_like(rest_rows)], axis=1).astype(BF16)

    def give(j):
        lanes = pl.ds(pl.multiple_of((S * HEADS_HERE + j) * HD, HD), HD)
        for d in range(1, SEQ):
            send(OB.at[j, peers[d - 1][1]], out.at[:, lanes], out_s.at[j, d - 1], out_r.at[j, d - 1], peers[d - 1])
        out[:, lanes] = OB[j, S]

    def take(j):
        for d in range(1, SEQ):
            src = lax.rem(S + SEQ - d, SEQ)
            lanes = pl.ds(pl.multiple_of((src * HEADS_HERE + j) * HD, HD), HD)
            arrived(out.at[:, lanes], out_s.at[j, d - 1], out_r.at[j, d - 1], peers[d - 1])

    def unpack(i, carry):
        pair = [RM[2 * i + n].astype(F32) for n in range(2)]
        rows = [jnp.concatenate([p[0:8], p[8:16]], axis=1) for p in pair]
        XR[pl.ds(pl.multiple_of(i * 16, 16), 16), :] = jnp.concatenate(rows, axis=0).astype(BF16)
        return carry

    def text_half(s):
        return T.at[s, 0:64]

    def image_half(s):
        return T.at[s, 64:128]

    def pass_on(parts, start, device):
        for i, part in enumerate(parts):
            send(part, part, tok_s.at[start + i], tok_r.at[start + i], device)

    def came(parts, start, device):
        for i, part in enumerate(parts):
            arrived(part, tok_s.at[start + i], tok_r.at[start + i], device)

    def near_came():
        tokens_arrived(s_xl, 0, d_xr)
        pass_on([text_half(s_xl)], 6, d_xr)
        tokens_arrived(s_xr, 2, d_xl)
        pass_on([image_half(s_xr), RM.at[s_xr]], 7, d_xl)

    def partner_came():
        tokens_arrived(s_yp, 4, d_yp)
        pass_on([T.at[s_yp], RM.at[s_yp]], 9, d_xr)
        pass_on([T.at[s_yp], RM.at[s_yp]], 11, d_xl)

    def opposite_came():
        came([text_half(s_xx)], 6, d_xr)
        came([image_half(s_xx), RM.at[s_xx]], 7, d_xl)
        pass_on([T.at[s_xx], RM.at[s_xx]], 13, d_yp)

    def all_came():
        tokens_arrived(o_xl, 9, d_xr)
        tokens_arrived(o_xr, 11, d_xl)
        tokens_arrived(o_xx, 13, d_yp)
        lax.fori_loop(0, 4, unpack, 0)

    OWN, PARTNER = 0, 1

    def hops(j, step):
        hop(j, OWN, step)
        hop(j, PARTNER, step)

    collect(0)
    first(0, OWN)
    for copy in loads[1:4]:
        copy.wait()
    for stream in range(2):
        row = jnp.zeros((2, D), F32)
        for i in range(mods.shape[0]):
            row = row + jnp.where(step_index[...] == i, mods[i, stream], 0.0)
        picked[stream] = row
    lax.fori_loop(0, 4, mod_text, 0)
    lax.fori_loop(0, 4, mod_image, 0)
    rest = modulate(image[64:72, :], 1)
    RM[S] = jnp.concatenate([rest[:, : D // 2], rest[:, D // 2 :]], axis=0).astype(BF16)
    where = lax.broadcasted_iota(jnp.int32, (8, TXT), 1)
    bias[...] = jnp.where(where < length[...], 0.0, -jnp.inf).astype(F32)
    collect(1)
    first(1, OWN)
    send_tokens(S, 0, d_xr)
    send_tokens(S, 2, d_xl)
    partner_rows(0)
    first(0, PARTNER)
    partner_rows(1)
    first(1, PARTNER)
    send_tokens(S, 4, d_yp)
    own_copies.append(a2a_start(2))
    V[:, :, HD:] = jnp.ones((HEADS_HERE, TOTAL, HD), BF16)
    hops(0, 1)
    hops(1, 1)
    flush(48)
    hops(0, 2)
    near_came()
    hops(1, 2)
    collect(2)
    partner_came()
    flush(48)
    hops(0, 3)
    first(2, OWN)
    opposite_came()
    hop(1, OWN, 3)
    partner_rows(2)
    first(2, PARTNER)
    hop(1, PARTNER, 3)
    hops(0, 4)
    for copy in loads[4:]:
        copy.wait()
    flush(48)
    sib_arrived(0)
    project(0, 0, near)
    hop(2, OWN, 1)
    project(0, 1, near)
    hop(1, OWN, 4)
    hop(2, PARTNER, 1)
    hop(1, PARTNER, 4)
    sib_arrived(1)
    project(1, 0, near)
    project(1, 1, near)
    hop(2, OWN, 2)
    all_came()
    project(0, 0, distant)
    hop(2, PARTNER, 2)
    project(0, 1, distant)
    attend(0)
    hop(2, OWN, 3)
    give(0)
    hop(2, PARTNER, 3)
    project(1, 0, distant)
    project(1, 1, distant)
    cross_arrived(2, (1, 2, 4, 5))
    sib_arrived(2, (0, 1, 2, 4, 5))
    project_some(2, 0, order[0:2])
    hop(2, OWN, 4)
    hop(2, PARTNER, 4)
    project_some(2, 1, order[0:2])
    attend(1)
    give(1)
    cross_arrived(2, (3, 6, 7))
    sib_arrived(2, (3, 6))
    project_some(2, 0, order[2:3])
    project_some(2, 1, order[2:3])
    sib_arrived(2, (7,))
    project_last(2)
    attend(2)
    give(2)
    flush(SEQ - 1)
    for j in range(HEADS_HERE):
        take(j)
    flush(0)


def cut(rows, text, image):
    text[0] = rows[0:TROWS, :]
    image[0] = rows[TROWS : TROWS + IROWS, :]


def on_device(text_tokens, image_tokens, weights, qk_gain, mod_table, text_lengths, time_index):
    wraw = jnp.transpose(weights, (1, 2, 0, 3))
    cosine, sine = rope_rows()
    vmem = pl.BlockSpec(memory_space=pltpu.VMEM)
    dma = pltpu.SemaphoreType.DMA
    n_tok = 15
    result = pl.pallas_call(
        kernel,
        out_shape=jax.ShapeDtypeStruct((144, D), BF16),
        in_specs=[pl.BlockSpec(memory_space=pltpu.HBM)] * 7 + [vmem] * 2,
        out_specs=vmem,
        scratch_shapes=[
            pltpu.VMEM(wraw.shape, BF16),
            pltpu.VMEM((2, 2, D), F32),
            pltpu.VMEM(text_tokens.shape[1:], BF16),
            pltpu.VMEM(image_tokens.shape[1:], BF16),
            pltpu.VMEM(mod_table.shape, F32),
            pltpu.VMEM((4, HD), F32),
            pltpu.VMEM((IMG, HD), F32),
            pltpu.VMEM((IMG, HD), F32),
            pltpu.VMEM((2, 3, 16, D), BF16),
            pltpu.VMEM((HEADS_HERE, 2, 2, D // 2, 3 * HD), BF16),
            pltpu.VMEM((HEADS_HERE, 2, 3, 128, HD), BF16),
            pltpu.VMEM((SEQ, 128, D), BF16),
            pltpu.VMEM((SEQ, 16, D // 2), BF16),
            pltpu.VMEM((SEQ * REST, D), BF16),
            pltpu.VMEM((HEADS_HERE, TOTAL, HD), BF16),
            pltpu.VMEM((HEADS_HERE, TOTAL, HD), BF16),
            pltpu.VMEM((HEADS_HERE, TOTAL, 2 * HD), BF16),
            pltpu.VMEM((HEADS_HERE, SEQ, 144, HD), BF16),
            pltpu.VMEM((8, TXT), F32),
            pltpu.VMEM((96, 128), BF16),
            pltpu.VMEM((TOTAL, 3 * HD), F32),
            dma((3, 7)), dma((3, 7)),
            dma((3,)), dma((3,)),
            dma((3, 2, 4)), dma((3, 2, 4)),
            dma((3, 2, 4)), dma((3, 2, 4)),
            dma((3, 2, 8)), dma((3, 2, 8)),
            dma((7,)), dma((7,)),
            dma((7,)), dma((7,)),
            dma((n_tok,)), dma((n_tok,)),
            dma((3, 7)), dma((3, 7)),
            dma((3,)),
            dma((7,)),
        ],
        compiler_params=pltpu.CompilerParams(
            collective_id=0, has_side_effects=True, vmem_limit_bytes=56 * 1024 * 1024
        ),
        cost_estimate=pl.CostEstimate(flops=9_500_000_000, bytes_accessed=30_000_000, transcendentals=3_600_000),
        name="joint_attention",
    )(
        wraw, text_tokens[0], image_tokens[0], mod_table, qk_gain.reshape(4, HD),
        jnp.asarray(cosine), jnp.asarray(sine), text_lengths.astype(jnp.int32).reshape(1, 1),
        time_index.astype(jnp.int32).reshape(1, 1),
    )
    return pl.pallas_call(
        cut,
        out_shape=(
            jax.ShapeDtypeStruct((1, TROWS, D), BF16),
            jax.ShapeDtypeStruct((1, IROWS, D), BF16),
        ),
        in_specs=[vmem],
        out_specs=(vmem, vmem),
        name="cut_outputs",
    )(result)


def solution(mesh):
    placed = (
        P("rep", "seq", None),
        P("rep", "seq", None),
        P(None, ("rep", "seq"), None, None),
        P(),
        P(),
        P("rep"),
        P("rep"),
    )
    return jax.shard_map(
        on_device,
        mesh=mesh,
        in_specs=placed,
        out_specs=(P("rep", "seq", None), P("rep", "seq", None)),
        check_vma=False,
    )
```

```python
import functools

import jax
import jax.numpy as jnp
import numpy as np
from jax import lax
from jax.experimental import pallas as pl
from jax.experimental.pallas import tpu as pltpu
from jax.sharding import PartitionSpec as P

D = 3072
HD = 128
GRID = 24
TXT = 512
IMG = GRID * GRID
TOTAL = TXT + IMG
SEQ = 8
NZ = 8
HEADS_HERE = 3
TROWS = TXT // SEQ
IROWS = IMG // SEQ
REST = IROWS - 64
WROWS = 12
KSTEP = 768
SCALE = float(HD**-0.5 * np.log2(np.e))
MESH = pl.DeviceIdType.MESH
BF16, F32 = jnp.bfloat16, jnp.float32


def rope_rows():
    pairs, still = HD // 2, HD // 16
    rows = (pairs - still) // 2
    cols = pairs - still - rows
    place = np.concatenate(
        [
            (np.arange(SEQ)[:, None] * IROWS + np.arange(64)[None, :]).reshape(-1),
            (np.arange(SEQ)[:, None] * IROWS + 64 + np.arange(REST)[None, :]).reshape(-1),
        ]
    )
    row_pos = (place // GRID).astype(np.float32)
    col_pos = (place % GRID).astype(np.float32)
    row_freq = (10000.0 ** (-np.arange(rows) / rows)).astype(np.float32)
    col_freq = (10000.0 ** (-np.arange(cols) / cols)).astype(np.float32)
    angles = np.concatenate(
        [
            np.zeros((IMG, still), np.float32),
            row_pos[:, None] * row_freq[None, :],
            col_pos[:, None] * col_freq[None, :],
        ],
        axis=1,
    )
    cosine = np.repeat(np.cos(angles), 2, axis=1)
    sine = np.repeat(np.sin(angles), 2, axis=1)
    sine[:, 0::2] *= -1.0
    return cosine.astype(np.float32), sine.astype(np.float32)


def kernel(
    wraw_hbm, text_hbm, image_hbm, mods_hbm, gains_hbm, cosine_hbm, sine_hbm, length, step_index,
    out,
    wraw, picked, text, image, mods, gains, cosine, sine, wsrc, W, A, T, RM, XR, Q, K, V, OB, bias, sel, acc,
    a2a_s, a2a_r, y_s, y_r, zr_s, zr_r, zl_s, zl_r, sib_s, sib_r, yc_s, yc_r, sc_s, sc_r, tok_s, tok_r, out_s, out_r, own_sem, load_sem,
):
    R, S = lax.axis_index("rep"), lax.axis_index("seq")
    core = lax.rem(R, 2)
    z = lax.rem(R // 2, NZ)
    yh = R // (2 * NZ)
    x = lax.rem(S, 4)
    yl = S // 4

    def rep_of(y, zz, c):
        return (y * NZ + zz) * 2 + c

    def up(dz):
        return lax.rem(z + dz + NZ, NZ)

    def xs(dx, row):
        return row * 4 + lax.rem(x + dx + 4, 4)

    sib = (rep_of(yh, z, 1 - core), S)
    zr = (rep_of(yh, up(1), core), S)
    zl = (rep_of(yh, up(-1), core), S)
    yp = (rep_of(1 - yh, z, core), S)
    peers = [(R, lax.rem(S + d, SEQ)) for d in range(1, SEQ)]
    s_yp, s_xr, s_xl, s_xx = xs(0, 1 - yl), xs(1, yl), xs(-1, yl), xs(2, yl)
    o_xr, o_xl, o_xx = xs(1, 1 - yl), xs(-1, 1 - yl), xs(2, 1 - yl)

    barrier = pltpu.get_barrier_semaphore()
    partners = [sib, zr, zl, yp] + peers
    for device in partners:
        pl.semaphore_signal(barrier, inc=1, device_id=device, device_id_type=MESH)
    loads = []
    for i, (far, near) in enumerate(
        [(wraw_hbm, wraw), (mods_hbm, mods), (text_hbm, text), (image_hbm, image), (gains_hbm, gains), (cosine_hbm, cosine), (sine_hbm, sine)]
    ):
        loads.append(pltpu.make_async_copy(far, near, load_sem.at[i]))
        loads[-1].start()

    loads[0].wait()
    for q in range(3):
        rows = wraw[:, q].astype(F32)
        for st in range(2):
            wsrc[st, q, 0:WROWS, :] = rows[:, st, :].astype(BF16)
    wsrc[:, :, WROWS:16, :] = jnp.zeros((2, 3, 16 - WROWS, D), BF16)

    pl.semaphore_wait(barrier, len(partners))

    pending = []

    def send(src, dst, ssem, rsem, device):
        copy = pltpu.make_async_remote_copy(
            src_ref=src, dst_ref=dst, send_sem=ssem, recv_sem=rsem, device_id=device, device_id_type=MESH
        )
        copy.start()
        pending.append(copy)

    def flush(keep):
        while len(pending) > keep:
            pending.pop(0).wait_send()

    def arrived(dst, ssem, rsem, device):
        pltpu.make_async_remote_copy(
            src_ref=dst, dst_ref=dst, send_sem=ssem, recv_sem=rsem, device_id=device, device_id_type=MESH
        ).wait_recv()

    def slot(j, s):
        return A.at[j, :, :, pl.ds(pl.multiple_of(s * 16, 16), 16), :]

    def piece(j, g):
        return wsrc.at[:, :, :, pl.ds(pl.multiple_of(g * (HEADS_HERE * HD) + j * HD, HD), HD)]

    def a2a_start(j):
        for d in range(1, SEQ):
            send(piece(j, peers[d - 1][1]), slot(j, S), a2a_s.at[j, d - 1], a2a_r.at[j, d - 1], peers[d - 1])
        copy = pltpu.make_async_copy(piece(j, S), slot(j, S), own_sem.at[j])
        copy.start()
        return copy

    own_copies = [a2a_start(0), a2a_start(1)]

    i96 = lax.broadcasted_iota(jnp.int32, (96, 128), 0)
    i128 = lax.broadcasted_iota(jnp.int32, (96, 128), 1)
    sel[...] = jnp.where(i128 == (i96 // WROWS) * 16 + lax.rem(i96, WROWS), 1.0, 0.0).astype(BF16)

    def modulate(rows, stream):
        v = rows.astype(F32)
        center = v - jnp.mean(v, axis=-1, keepdims=True)
        spread = jnp.mean(center * center, axis=-1, keepdims=True)
        normed = center * lax.rsqrt(spread + 1e-06)
        return normed * (1.0 + picked[stream, 1:2, :]) + picked[stream, 0:1, :]

    def mod_text(i, carry):
        rows = pl.ds(pl.multiple_of(i * 16, 16), 16)
        T[S, rows, :] = modulate(text[rows, :], 0).astype(BF16)
        return carry

    def mod_image(i, carry):
        rows = pl.ds(pl.multiple_of(i * 16, 16), 16)
        T[S, pl.ds(pl.multiple_of(64 + i * 16, 16), 16), :] = modulate(image[rows, :], 1).astype(BF16)
        return carry

    def send_tokens(s, first, device):
        send(T.at[s], T.at[s], tok_s.at[first], tok_r.at[first], device)
        send(RM.at[s], RM.at[s], tok_s.at[first + 1], tok_r.at[first + 1], device)

    def tokens_arrived(s, first, device):
        arrived(T.at[s], tok_s.at[first], tok_r.at[first], device)
        arrived(RM.at[s], tok_s.at[first + 1], tok_r.at[first + 1], device)

    d_yp, d_xr, d_xl = (R, s_yp), (R, s_xr), (R, s_xl)
    def rows_of(zz, c):
        return pl.ds(pl.multiple_of((zz * 2 + c) * 96, 32), 96)

    def block(j, y, zz, c):
        return W.at[j, :, y, rows_of(zz, c), :]

    def half(j, st, y, zz, c):
        return W.at[j, st, y, rows_of(zz, c), :]

    def gather_rows(j):
        own_copies[j].wait()
        for d in range(1, SEQ):
            src = lax.rem(S + SEQ - d, SEQ)
            arrived(slot(j, src), a2a_s.at[j, d - 1], a2a_r.at[j, d - 1], peers[d - 1])
        for st in range(2):
            rows = jnp.concatenate([A[j, st, q] for q in range(3)], axis=1)
            W[j, st, yh, rows_of(z, core), :] = jnp.dot(sel[...], rows, preferred_element_type=F32).astype(BF16)

    yy = [yh, 1 - yh]

    def split(j, w):
        return (j, w) == (2, 1)

    def ring_block(j, w, zz):
        return half(j, 0, yy[w], zz, core) if split(j, w) else block(j, yy[w], zz, core)

    def sib_send(j, w, k, zz):
        b = ring_block(j, w, zz) if k else block(j, yy[w], zz, core)
        send(b, b, sib_s.at[j, w, k], sib_r.at[j, w, k], sib)

    def first(j, w):
        b = ring_block(j, w, z)
        send(b, b, zr_s.at[j, w, 0], zr_r.at[j, w, 0], zr)
        send(b, b, zl_s.at[j, w, 0], zl_r.at[j, w, 0], zl)
        sib_send(j, w, 0, z)

    def collect(j):
        gather_rows(j)
        b = block(j, yh, z, core)
        send(b, b, y_s.at[j], y_r.at[j], yp)

    def partner_rows(j):
        arrived(block(j, 1 - yh, z, core), y_s.at[j], y_r.at[j], yp)

    def cross(j, w, k, zz):
        if split(j, 1) and w == 0:
            b = half(j, 1, yh, zz, core)
            send(b, b, yc_s.at[k - 1], yc_r.at[k - 1], yp)

    def cross_arrived(j, ks):
        if not split(j, 1):
            return
        for k, dz in ((1, -1), (2, -2), (3, -3), (4, 1), (5, 2), (6, 3), (7, 4)):
            if k not in ks:
                continue
            b = half(j, 1, 1 - yh, up(dz), core)
            arrived(b, yc_s.at[k - 1], yc_r.at[k - 1], yp)
            send(b, b, sc_s.at[k - 1], sc_r.at[k - 1], sib)

    def hop(j, w, step):
        if step < 4:
            for sems, sign, k in (((zr_s, zr_r, zr), -1, step), ((zl_s, zl_r, zl), 1, step + 3)):
                b = ring_block(j, w, up(sign * step))
                arrived(b, sems[0].at[j, w, step - 1], sems[1].at[j, w, step - 1], sems[2])
                f = b if step < 3 else half(j, 0 if sign < 0 else 1, yy[w], up(sign * step), core)
                if step < 3 or sign < 0 or not split(j, w):
                    send(f, f, sems[0].at[j, w, step], sems[1].at[j, w, step], sems[2])
                sib_send(j, w, k, up(sign * step))
                cross(j, w, k, up(sign * step))
        else:
            arrived(half(j, 0, yy[w], up(4), core), zr_s.at[j, w, 3], zr_r.at[j, w, 3], zr)
            if not split(j, w):
                arrived(half(j, 1, yy[w], up(4), core), zl_s.at[j, w, 3], zl_r.at[j, w, 3], zl)
            sib_send(j, w, 7, up(4))
            cross(j, w, 7, up(4))

    def sib_arrived(j, ks=range(8)):
        for w in range(2):
            for k, dz in enumerate((0, -1, -2, -3, 1, 2, 3, 4)):
                if k not in ks:
                    continue
                whole = block(j, yy[w], up(dz), 1 - core)
                b = half(j, 0, yy[w], up(dz), 1 - core) if k and split(j, w) else whole
                arrived(b, sib_s.at[j, w, k], sib_r.at[j, w, k], sib)
                if k and split(j, w):
                    b = half(j, 1, yy[w], up(dz), 1 - core)
                    arrived(b, sc_s.at[k - 1], sc_r.at[k - 1], sib)

    def prepare(j, st, rows, places, start):
        def table(ref):
            return jnp.concatenate([ref[pl.ds(at - start, n), :] for at, n in places], axis=0)

        for part, store in ((0, Q), (1, K), (2, V)):
            v = rows[:, part * HD : (part + 1) * HD]
            if part < 2:
                power = jnp.mean(v * v, axis=-1, keepdims=True)
                v = v * lax.rsqrt(power + 1e-06) * gains[2 * st + part : 2 * st + part + 1, :]
                if st == 1:
                    even = lax.rem(lax.broadcasted_iota(jnp.int32, v.shape, 1), 2) == 0
                    turned = jnp.where(even, pltpu.roll(v, HD - 1, 1), pltpu.roll(v, 1, 1))
                    v = v * table(cosine) + turned * table(sine)
            v = v.astype(BF16)
            done = 0
            for at, n in places:
                store[j, pl.ds(at, n), 0:HD] = v[done : done + n]
                done += n

    near, distant = (S, s_xl, s_xr, s_yp, s_xx), (o_xl, o_xr, o_xx)

    def project(j, st, slots):
        base = TXT * st
        lhs = [T[s, 64 * st : 64 * st + 64, :] for s in slots]
        places = [(pl.multiple_of(base + s * 64, 64), 64) for s in slots]
        if st == 1 and slots is distant:
            lhs.append(XR[...])
            places.append((TXT + 512, 64))
        rows = jnp.dot(
            jnp.concatenate(lhs, axis=0), W[j, st].reshape(D, 3 * HD), preferred_element_type=F32
        )
        prepare(j, st, rows, places, TXT)

    def partial(j, st, quarters):
        total = None
        for q in quarters:
            cols = [pl.ds(pl.multiple_of(y * (D // 2) + q * 384, 128), 384) for y in range(2)]
            lhs = jnp.concatenate(
                [T[:, 64 * st : 64 * st + 64, c].reshape(SEQ * 64, 384) for c in cols], axis=1
            )
            if st == 1:
                lhs = jnp.concatenate([lhs, jnp.concatenate([XR[:, c] for c in cols], axis=1)], axis=0)
            rhs = jnp.concatenate([W[j, st, y, pl.ds(pl.multiple_of(q * 384, 128), 384), :] for y in range(2)], axis=0)
            term = jnp.dot(lhs, rhs, preferred_element_type=F32)
            total = term if total is None else total + term
        return total

    quarter = z // 2

    def project_some(j, st, quarters):
        at, n = ((0, TXT), (TXT, IMG))[st]
        total = partial(j, st, quarters)
        acc[at : at + n, :] = total if len(quarters) == 2 else acc[at : at + n, :] + total

    side = 2 * lax.rem(z, 2) - 1
    order = [quarter, lax.rem(quarter + side + 4, 4), lax.rem(quarter - side + 4, 4), lax.rem(quarter + 2, 4)]

    def project_last(j):
        for st, at, n in ((0, 0, TXT), (1, TXT, IMG)):
            rows = acc[at : at + n, :] + partial(j, st, order[3:])
            prepare(j, st, rows, [(at, n)], TXT)

    def attend_rows(j, q):
        scores = lax.dot_general(q, K[j], (((1,), (1,)), ((), ())), preferred_element_type=F32)
        scores = jnp.concatenate([scores[:, :TXT] + bias[0:1, :], scores[:, TXT:]], axis=1)
        weight = jnp.exp2((scores - jnp.max(scores, axis=-1, keepdims=True)) * SCALE)
        mixed = jnp.dot(weight.astype(BF16), V[j], preferred_element_type=F32)
        return mixed[:, :HD] / mixed[:, HD:]

    def attend(j):
        first = attend_rows(j, Q[j, 0:544, :])
        second = attend_rows(j, Q[j, 544:1088, :])
        OB[j, :, 0:64, :] = first[0:512].astype(BF16).reshape(SEQ, 64, HD)
        image_rows = jnp.concatenate([first[512:544], second[0:480]], axis=0)
        OB[j, :, 64:128, :] = image_rows.astype(BF16).reshape(SEQ, 64, HD)
        rest_rows = second[480:544].reshape(SEQ, REST, HD)
        OB[j, :, 128:144, :] = jnp.concatenate([rest_rows, jnp.zeros_like(rest_rows)], axis=1).astype(BF16)

    def give(j):
        lanes = pl.ds(pl.multiple_of((S * HEADS_HERE + j) * HD, HD), HD)
        for d in range(1, SEQ):
            send(OB.at[j, peers[d - 1][1]], out.at[:, lanes], out_s.at[j, d - 1], out_r.at[j, d - 1], peers[d - 1])
        out[:, lanes] = OB[j, S]

    def take(j):
        for d in range(1, SEQ):
            src = lax.rem(S + SEQ - d, SEQ)
            lanes = pl.ds(pl.multiple_of((src * HEADS_HERE + j) * HD, HD), HD)
            arrived(out.at[:, lanes], out_s.at[j, d - 1], out_r.at[j, d - 1], peers[d - 1])

    def unpack(i, carry):
        pair = [RM[2 * i + n].astype(F32) for n in range(2)]
        rows = [jnp.concatenate([p[0:8], p[8:16]], axis=1) for p in pair]
        XR[pl.ds(pl.multiple_of(i * 16, 16), 16), :] = jnp.concatenate(rows, axis=0).astype(BF16)
        return carry

    def text_half(s):
        return T.at[s, 0:64]

    def image_half(s):
        return T.at[s, 64:128]

    def pass_on(parts, start, device):
        for i, part in enumerate(parts):
            send(part, part, tok_s.at[start + i], tok_r.at[start + i], device)

    def came(parts, start, device):
        for i, part in enumerate(parts):
            arrived(part, tok_s.at[start + i], tok_r.at[start + i], device)

    def near_came():
        tokens_arrived(s_xl, 0, d_xr)
        pass_on([text_half(s_xl)], 6, d_xr)
        tokens_arrived(s_xr, 2, d_xl)
        pass_on([image_half(s_xr), RM.at[s_xr]], 7, d_xl)

    def partner_came():
        tokens_arrived(s_yp, 4, d_yp)
        pass_on([T.at[s_yp], RM.at[s_yp]], 9, d_xr)
        pass_on([T.at[s_yp], RM.at[s_yp]], 11, d_xl)

    def opposite_came():
        came([text_half(s_xx)], 6, d_xr)
        came([image_half(s_xx), RM.at[s_xx]], 7, d_xl)
        pass_on([T.at[s_xx], RM.at[s_xx]], 13, d_yp)

    def all_came():
        tokens_arrived(o_xl, 9, d_xr)
        tokens_arrived(o_xr, 11, d_xl)
        tokens_arrived(o_xx, 13, d_yp)
        lax.fori_loop(0, 4, unpack, 0)

    OWN, PARTNER = 0, 1

    def hops(j, step):
        hop(j, OWN, step)
        hop(j, PARTNER, step)

    collect(0)
    first(0, OWN)
    for copy in loads[1:4]:
        copy.wait()
    for stream in range(2):
        row = jnp.zeros((2, D), F32)
        for i in range(mods.shape[0]):
            row = row + jnp.where(step_index[...] == i, mods[i, stream], 0.0)
        picked[stream] = row
    lax.fori_loop(0, 4, mod_text, 0)
    lax.fori_loop(0, 4, mod_image, 0)
    rest = modulate(image[64:72, :], 1)
    RM[S] = jnp.concatenate([rest[:, : D // 2], rest[:, D // 2 :]], axis=0).astype(BF16)
    where = lax.broadcasted_iota(jnp.int32, (8, TXT), 1)
    bias[...] = jnp.where(where < length[...], 0.0, -jnp.inf).astype(F32)
    collect(1)
    first(1, OWN)
    send_tokens(S, 0, d_xr)
    send_tokens(S, 2, d_xl)
    partner_rows(0)
    first(0, PARTNER)
    partner_rows(1)
    first(1, PARTNER)
    send_tokens(S, 4, d_yp)
    own_copies.append(a2a_start(2))
    V[:, :, HD:] = jnp.ones((HEADS_HERE, TOTAL, HD), BF16)
    hops(0, 1)
    hops(1, 1)
    flush(48)
    hops(0, 2)
    near_came()
    hops(1, 2)
    collect(2)
    partner_came()
    flush(48)
    hops(0, 3)
    first(2, OWN)
    opposite_came()
    hop(1, OWN, 3)
    partner_rows(2)
    first(2, PARTNER)
    hop(1, PARTNER, 3)
    hops(0, 4)
    for copy in loads[4:]:
        copy.wait()
    flush(48)
    sib_arrived(0)
    project(0, 0, near)
    hop(2, OWN, 1)
    project(0, 1, near)
    hop(1, OWN, 4)
    hop(2, PARTNER, 1)
    hop(1, PARTNER, 4)
    sib_arrived(1)
    project(1, 0, near)
    project(1, 1, near)
    hop(2, OWN, 2)
    all_came()
    project(0, 0, distant)
    hop(2, PARTNER, 2)
    project(0, 1, distant)
    attend(0)
    hop(2, OWN, 3)
    give(0)
    hop(2, PARTNER, 3)
    project(1, 0, distant)
    project(1, 1, distant)
    hop(2, OWN, 4)
    hop(2, PARTNER, 4)
    attend(1)
    give(1)
    cross_arrived(2, (1, 2, 4, 5))
    sib_arrived(2, (0, 1, 2, 4, 5))
    project_some(2, 0, order[0:2])
    project_some(2, 1, order[0:2])
    cross_arrived(2, (3, 6, 7))
    sib_arrived(2, (3, 6))
    project_some(2, 0, order[2:3])
    project_some(2, 1, order[2:3])
    sib_arrived(2, (7,))
    project_last(2)
    attend(2)
    give(2)
    flush(SEQ - 1)
    for j in range(HEADS_HERE):
        take(j)
    flush(0)


def cut(rows, text, image):
    text[0] = rows[0:TROWS, :]
    image[0] = rows[TROWS : TROWS + IROWS, :]


def on_device(text_tokens, image_tokens, weights, qk_gain, mod_table, text_lengths, time_index):
    wraw = jnp.transpose(weights, (1, 2, 0, 3))
    cosine, sine = rope_rows()
    vmem = pl.BlockSpec(memory_space=pltpu.VMEM)
    dma = pltpu.SemaphoreType.DMA
    n_tok = 15
    result = pl.pallas_call(
        kernel,
        out_shape=jax.ShapeDtypeStruct((144, D), BF16),
        in_specs=[pl.BlockSpec(memory_space=pltpu.HBM)] * 7 + [vmem] * 2,
        out_specs=vmem,
        scratch_shapes=[
            pltpu.VMEM(wraw.shape, BF16),
            pltpu.VMEM((2, 2, D), F32),
            pltpu.VMEM(text_tokens.shape[1:], BF16),
            pltpu.VMEM(image_tokens.shape[1:], BF16),
            pltpu.VMEM(mod_table.shape, F32),
            pltpu.VMEM((4, HD), F32),
            pltpu.VMEM((IMG, HD), F32),
            pltpu.VMEM((IMG, HD), F32),
            pltpu.VMEM((2, 3, 16, D), BF16),
            pltpu.VMEM((HEADS_HERE, 2, 2, D // 2, 3 * HD), BF16),
            pltpu.VMEM((HEADS_HERE, 2, 3, 128, HD), BF16),
            pltpu.VMEM((SEQ, 128, D), BF16),
            pltpu.VMEM((SEQ, 16, D // 2), BF16),
            pltpu.VMEM((SEQ * REST, D), BF16),
            pltpu.VMEM((HEADS_HERE, TOTAL, HD), BF16),
            pltpu.VMEM((HEADS_HERE, TOTAL, HD), BF16),
            pltpu.VMEM((HEADS_HERE, TOTAL, 2 * HD), BF16),
            pltpu.VMEM((HEADS_HERE, SEQ, 144, HD), BF16),
            pltpu.VMEM((8, TXT), F32),
            pltpu.VMEM((96, 128), BF16),
            pltpu.VMEM((TOTAL, 3 * HD), F32),
            dma((3, 7)), dma((3, 7)),
            dma((3,)), dma((3,)),
            dma((3, 2, 4)), dma((3, 2, 4)),
            dma((3, 2, 4)), dma((3, 2, 4)),
            dma((3, 2, 8)), dma((3, 2, 8)),
            dma((7,)), dma((7,)),
            dma((7,)), dma((7,)),
            dma((n_tok,)), dma((n_tok,)),
            dma((3, 7)), dma((3, 7)),
            dma((3,)),
            dma((7,)),
        ],
        compiler_params=pltpu.CompilerParams(
            collective_id=0, has_side_effects=True, vmem_limit_bytes=56 * 1024 * 1024
        ),
        cost_estimate=pl.CostEstimate(flops=9_500_000_000, bytes_accessed=30_000_000, transcendentals=3_600_000),
        name="joint_attention",
    )(
        wraw, text_tokens[0], image_tokens[0], mod_table, qk_gain.reshape(4, HD),
        jnp.asarray(cosine), jnp.asarray(sine), text_lengths.astype(jnp.int32).reshape(1, 1),
        time_index.astype(jnp.int32).reshape(1, 1),
    )
    return pl.pallas_call(
        cut,
        out_shape=(
            jax.ShapeDtypeStruct((1, TROWS, D), BF16),
            jax.ShapeDtypeStruct((1, IROWS, D), BF16),
        ),
        in_specs=[vmem],
        out_specs=(vmem, vmem),
        name="cut_outputs",
    )(result)


def solution(mesh):
    placed = (
        P("rep", "seq", None),
        P("rep", "seq", None),
        P(None, ("rep", "seq"), None, None),
        P(),
        P(),
        P("rep"),
        P("rep"),
    )
    return jax.shard_map(
        on_device,
        mesh=mesh,
        in_specs=placed,
        out_specs=(P("rep", "seq", None), P("rep", "seq", None)),
        check_vma=False,
    )
```
